512 devices in a mesh: ri: 64 (over x, y_lo, z), bas: 8 (over y_hi, core).
Axes of the slice: x: 4, y: 8 (y_hi: 4, y_lo: 2; y = y_hi * 2 + y_lo), z: 8, core: 2. Of those that a mesh axis runs over, the one named last changes fastest.
Arguments:
- three_centre: bfloat16 [64, 8, 32, 2, 128, 128], P('ri', 'bas'), may hold values from -0.5 to 0.5
- slot_index: int32 [64, 8, 32, 3], P('ri', 'bas'), may hold values from 0 to 15, as said below
- slot_count: int32 [64, 8], P('ri', 'bas'), may hold values from 8 to 32, as said below
- panel_last: bfloat16 [2048, 512], P(('ri', 'bas')), may hold values from -0.125 to 0.125
- panel_prev: bfloat16 [2048, 512], P(('ri', 'bas')), may hold values from -0.125 to 0.125
- panel_older: bfloat16 [2048, 512], P(('ri', 'bas')), may hold values from -0.125 to 0.125
Outputs:
- exchange: float32 [8, 64, 4, 2048], P('bas', 'ri')
The draws below stay inside these ranges and needn't reach their ends.
Inputs may be any that keep to these rules, and one draw needn't show every extreme that they name: `slot_index`: within one device the 32 slots name distinct triples; first column below 1, second below 2, third below 16. Slots from slot_count on are unused. `slot_count`: in every group of devices that share an ri index, one device uses all 32 slots.
All inputs are finite; a program needn't handle non-finite values.
Results may differ from the reference program's by a relative error of at most 0.0011.
Values may be sent and summed in bfloat16 or wider, within the bound.
A program may use at most 128 MiB of HBM per device.

```python
import jax
import jax.numpy as jnp
from jax import lax

BLK = 128
NBLK = 16
OCC = 512
RB = 2
P_DEV = 2
SLOTS = 32
NBAS = 2048
GRID_RI = 64
GRID_BAS = 8
OWN_BLK = 2
OWN_ROWS = 4


def block_pattern(key):
    key = jax.random.fold_in(key, 7)
    key_order, key_count, key_fullest = jax.random.split(key, 3)
    owned_blocks = NBLK // GRID_BAS
    candidates = P_DEV // RB * owned_blocks * NBLK
    device_keys = jax.random.split(key_order, GRID_RI * GRID_BAS)

    def device_order(device_key):
        rest = jax.random.permutation(device_key, candidates - 2)[:SLOTS - 2] + 1
        ends = jnp.array([candidates - 1, 0], dtype=rest.dtype)
        return jnp.concatenate([ends, rest])
    orders = jax.vmap(device_order)(device_keys)
    ri_block = orders // (owned_blocks * NBLK)
    remain = orders % (owned_blocks * NBLK)
    row_block = remain // NBLK
    column_block = remain % NBLK
    slot_ids = jnp.stack([ri_block, row_block, column_block], -1).reshape(GRID_RI, GRID_BAS, SLOTS, 3).astype(jnp.int32)
    counts = jax.random.randint(key_count, (GRID_RI, GRID_BAS), SLOTS // 4, SLOTS // 2 + 1)
    fullest = jax.random.randint(key_fullest, (GRID_RI,), 0, GRID_BAS)
    counts = jnp.where(jnp.arange(GRID_BAS)[None, :] == fullest[:, None], SLOTS, counts)
    return (slot_ids, counts.astype(jnp.int32))


def draw_slot_index(key, part):
    return block_pattern(key)[0]


def draw_slot_count(key, part):
    return block_pattern(key)[1]


def levels(own_key, dims, cuts, smallest, top_value):
    factor_of = 1.0
    for dim, blocks in cuts:
        draws = jax.random.uniform(jax.random.fold_in(jax.random.fold_in(own_key, 6), dim), (blocks,), jnp.float32, smallest / len(cuts), top_value / len(cuts))
        factor_of = factor_of * jnp.repeat(jnp.exp(draws), dims[dim] // blocks).reshape((-1,) + (1,) * (len(dims) - 1 - dim))
    return factor_of


def normal_values(own_key, extent, width, most, cuts=(), kind=jnp.bfloat16):
    loudness = levels(own_key, extent, cuts, -0.22, 0.18) if cuts else 1.0
    result = jax.random.normal(own_key, extent, jnp.float32) * width * loudness
    return jnp.minimum(jnp.maximum(result, -most), most).astype(kind)


def setup_inputs(seed: int = 0) -> dict:
    streams_of = jax.random.split(jax.random.key(seed), 7)
    return {
        "three_centre": normal_values(streams_of[0], (GRID_RI, GRID_BAS, SLOTS, RB, BLK, BLK), BLK ** -0.5, 0.5, ((0, 64), (1, 8))),
        "slot_index": draw_slot_index(jax.random.fold_in(streams_of[6], 71), 0),
        "slot_count": draw_slot_count(jax.random.fold_in(streams_of[6], 71), 0),
        "panel_last": normal_values(streams_of[3], (NBAS, OCC), NBAS ** -0.5, 0.125, ((0, 512),)),
        "panel_prev": normal_values(streams_of[4], (NBAS, OCC), NBAS ** -0.5, 0.125, ((0, 512),)),
        "panel_older": normal_values(streams_of[5], (NBAS, OCC), NBAS ** -0.5, 0.125, ((0, 512),)),
    }


def predict_panel(panel_last, panel_prev, panel_older):
    mixed_sum = 2.5 * panel_last.astype(jnp.float32) - 2.0 * panel_prev.astype(jnp.float32) + 0.5 * panel_older.astype(jnp.float32)
    return mixed_sum.astype(jnp.bfloat16)


def reference(three_centre, slot_index, slot_count, panel_last, panel_prev, panel_older):
    predicted = predict_panel(panel_last, panel_prev, panel_older)
    zero_index = jnp.int32(0)

    def slot_step(half_rows, item):
        block, slot_ids, live_flag, owner = item
        panel_rows = lax.dynamic_slice_in_dim(predicted, (slot_ids[2] * BLK).astype(jnp.int32), BLK, 0)
        term = jnp.einsum("pmn,ni->pmi", block.astype(jnp.float32), panel_rows.astype(jnp.float32), precision=lax.Precision.HIGHEST) * live_flag
        row_start = (slot_ids[0] * RB).astype(jnp.int32)
        col_start = ((owner * OWN_BLK + slot_ids[1]) * BLK).astype(jnp.int32)
        corner = (row_start, col_start, zero_index)
        current = lax.dynamic_slice(half_rows, corner, (RB, BLK, OCC))
        return lax.dynamic_update_slice(half_rows, current + term, corner), None

    def ri_step(running_sum, inputs):
        blocks, slot_ids, live_count = inputs
        owners = jnp.repeat(jnp.arange(GRID_BAS, dtype=jnp.int32), SLOTS)
        live_flags = (jnp.arange(SLOTS, dtype=jnp.int32)[None, :] < live_count[:, None]).astype(jnp.float32).reshape(-1)
        start_rows = jnp.zeros((P_DEV, NBAS, OCC), jnp.float32)
        items = (blocks.reshape(GRID_BAS * SLOTS, RB, BLK, BLK), slot_ids.reshape(GRID_BAS * SLOTS, 3), live_flags, owners)
        half_rows, _ = lax.scan(slot_step, start_rows, items)
        rounded = lax.optimization_barrier(half_rows.astype(jnp.bfloat16)).astype(jnp.float32)
        product = jnp.einsum("pmi,pli->ml", rounded, rounded, precision=lax.Precision.HIGHEST)
        return running_sum + product, None

    exchange_sum, _ = lax.scan(ri_step, jnp.zeros((NBAS, NBAS), jnp.float32), (three_centre, slot_index, slot_count))
    return (-0.25 * exchange_sum).reshape(GRID_BAS, GRID_RI, OWN_ROWS, NBAS)
```

```python
import jax
import jax.numpy as jnp
from jax import lax
from jax.experimental import pallas as pl
from jax.experimental.pallas import tpu as pltpu
from jax.sharding import PartitionSpec as P

MESH = pl.DeviceIdType.MESH
BF16, F32 = jnp.bfloat16, jnp.float32

BLK = 128
NBLK = 16
OCC = 512
RB = 2
SLOTS = 32
ROWS = 256
NX, NYL, NZ, NYH, NC = 4, 2, 8, 4, 2
NRI = NX * NYL * NZ
NBAS = NYH * NC
NJ = 2
LW = OCC // NJ
XR = ROWS // NX
GW = 512


def kernel(
    inv_ref, live_ref, t_hbm, last_ref, prev_ref, older_ref, out_ref,
    t_v, dense, pred, heads, panel, half, part, sent, got, shareA, shareB, landA, landB,
    t_sem,
    s_head, r_head, s_z, r_z, s_xy, r_xy, s_core, r_core,
    s_y, r_y, s_hc, r_hc, s_x, r_x, s_fa, r_fa, s_fb, r_fb,
):
    ri, bas = lax.axis_index("ri"), lax.axis_index("bas")
    x, yl, z = ri // (NYL * NZ), (ri // NZ) % NYL, ri % NZ
    yh, core = bas // NC, bas % NC
    line = x * NYL + yl
    me = (ri, bas)
    other = (ri, yh * NC + 1 - core)

    def at(x_, yl_, z_):
        return (x_ * NYL + yl_) * NZ + z_

    def bas_peer(i):
        return (ri, (bas + i) % NBAS)

    def z_peer(i):
        return (at(x, yl, (z + i) % NZ), bas)

    def xy_peer(i):
        return (at((x + i // NYL) % NX, (yl + i % NYL) % NYL, z), bas)

    def yz_peer(i):
        return (at(x, (yl + i // NZ) % NYL, (z + i % NZ) % NZ), bas)

    def y_peer(i):
        return (ri, ((yh + i) % NYH) * NC + core)

    started = []

    def send(src, dst, ssem, rsem, dev):
        copy = pltpu.make_async_remote_copy(
            src_ref=src, dst_ref=dst, send_sem=ssem, recv_sem=rsem, device_id=dev, device_id_type=MESH
        )
        copy.start()
        started.append(copy)

    def arrive(dst, ssem, rsem):
        pltpu.make_async_remote_copy(
            src_ref=dst, dst_ref=dst, send_sem=ssem, recv_sem=rsem, device_id=other, device_id_type=MESH
        ).wait_recv()

    t_copy = pltpu.make_async_copy(t_hbm, t_v, t_sem)
    t_copy.start()

    peers = [bas_peer(i) for i in range(1, NBAS)]
    peers += [yz_peer(i) for i in range(1, NYL * NZ)]
    peers += [xy_peer(i) for i in range(NYL, NX * NYL)]
    barrier = pltpu.get_barrier_semaphore()
    for dev in peers:
        pl.semaphore_signal(barrier, inc=1, device_id=dev, device_id_type=MESH)

    mixed = (
        2.5 * last_ref[...].astype(F32) - 2.0 * prev_ref[...].astype(F32) + 0.5 * older_ref[...].astype(F32)
    ).astype(BF16)
    pred[...] = mixed.astype(F32)
    heads[bas] = mixed.astype(F32)
    pl.semaphore_wait(barrier, len(peers))

    for i in range(1, NBAS):
        send(pred, heads.at[bas], s_head.at[i], r_head.at[i], bas_peer(i))

    t_copy.wait()
    for u in range(ROWS // BLK):
        for v in range(NBLK):
            k = u * NBLK + v
            block = t_v[inv_ref[k]]
            block = jnp.where(live_ref[k] != 0, block, jnp.zeros_like(block))
            dense[:, pl.ds(u * BLK, BLK), pl.ds(v * BLK, BLK)] = block

    for i in range(1, NBAS):
        arrive(heads.at[(bas - i + NBAS) % NBAS], s_head.at[i], r_head.at[i])
    rows = jnp.concatenate([heads[core * 4 + i] for i in range(4)], axis=0).astype(BF16)
    for j in range(NJ):
        panel[j, ri, core] = rows[:, j * LW : (j + 1) * LW]

    mine = panel.at[:, ri, core]
    for i in range(1, NZ):
        send(mine, mine, s_z.at[i], r_z.at[i], z_peer(i))
    for i in range(1, NZ):
        src = at(x, yl, (z - i + NZ) % NZ)
        arrive(panel.at[:, src, core], s_z.at[i], r_z.at[i])

    for j in range(NJ):
        mine = panel.at[j, pl.ds(line * NZ, NZ), core]
        for i in range(1, NX * NYL):
            send(mine, mine, s_xy.at[j, i], r_xy.at[j, i], xy_peer(i))

    left, right = (yh - 1 + NYH) % NYH, (yh + 1) % NYH
    across = (yh + 2) % NYH

    def product(j, p):
        columns = panel[j].reshape(NBLK * BLK, LW)
        return jnp.dot(dense[p], columns, preferred_element_type=F32).astype(BF16)

    for j in range(NJ):
        for i in range(1, NX * NYL):
            src = ((x - i // NYL + NX) % NX) * NYL + (yl + i % NYL) % NYL
            arrive(panel.at[j, pl.ds(src * NZ, NZ), core], s_xy.at[j, i], r_xy.at[j, i])
        mine = panel.at[j, :, core]
        send(mine, mine, s_core.at[j], r_core.at[j], other)
        arrive(panel.at[j, :, 1 - core], s_core.at[j], r_core.at[j])
        for p in range(RB):
            half[bas, j, p] = product(j, p)
        mine = half.at[bas, j]
        send(mine, mine, s_y.at[j, 0], r_y.at[j, 0], y_peer(1))
        send(mine, mine, s_y.at[j, 1], r_y.at[j, 1], y_peer(3))
        send(mine, mine, s_hc.at[j, 0], r_hc.at[j, 0], other)

    def block(yh_):
        return half.at[yh_ * NC + core]

    def far_block(yh_):
        return half.at[yh_ * NC + 1 - core]

    def multiply(g, yh_):
        for c in range(NC):
            total = jnp.zeros((ROWS, ROWS), F32)
            for j in range(NJ):
                for p in range(RB):
                    total += lax.dot_general(
                        half[bas, j, p], half[yh_ * NC + c, j, p], (((1,), (1,)), ((), ())),
                        preferred_element_type=F32,
                    )
            part[g, :, c * ROWS : (c + 1) * ROWS] = total
            sent[g, :, c * ROWS : (c + 1) * ROWS] = total.astype(BF16)
        for i in range(1, NX):
            x_ = (x + i) % NX
            send(sent.at[g, pl.ds(x_ * XR, XR)], got.at[g, i], s_x.at[g, i], r_x.at[g, i], (at(x_, yl, z), bas))

    def sum_x(g):
        total = part[g, pl.ds(x * XR, XR), :]
        for i in range(1, NX):
            arrive(got.at[g, i], s_x.at[g, i], r_x.at[g, i])
        for i in range(1, NX):
            total += got[g, i].astype(F32)
        return total

    for j in range(NJ):
        arrive(far_block(yh).at[j], s_hc.at[j, 0], r_hc.at[j, 0])
    multiply(0, yh)

    for j in range(NJ):
        mine = block(left).at[j]
        arrive(mine, s_y.at[j, 0], r_y.at[j, 0])
        send(mine.at[0], mine.at[0], s_y.at[j, 2], r_y.at[j, 2], y_peer(1))
        send(mine, mine, s_hc.at[j, 1], r_hc.at[j, 1], other)
        mine = block(right).at[j]
        arrive(mine, s_y.at[j, 1], r_y.at[j, 1])
        send(mine.at[1], mine.at[1], s_y.at[j, 3], r_y.at[j, 3], y_peer(3))
        send(mine, mine, s_hc.at[j, 2], r_hc.at[j, 2], other)
    for g, yh_ in ((1, left), (2, right)):
        for j in range(NJ):
            arrive(far_block(yh_).at[j], s_hc.at[j, g], r_hc.at[j, g])
        multiply(g, yh_)

    here = yl * NZ + z
    for g in range(3):
        total = sum_x(g)
        for i in range(NYL * NZ):
            shareA[i, :, g * GW : (g + 1) * GW] = total[i * 4 : i * 4 + 4, :]
    landA[here] = shareA[here]
    for i in range(1, NYL * NZ):
        there = ((yl + i // NZ) % NYL) * NZ + (z + i % NZ) % NZ
        send(shareA.at[there], landA.at[here], s_fa.at[i], r_fa.at[i], yz_peer(i))

    for j in range(NJ):
        mine = block(across).at[j]
        arrive(mine.at[0], s_y.at[j, 2], r_y.at[j, 2])
        arrive(mine.at[1], s_y.at[j, 3], r_y.at[j, 3])
        send(mine, mine, s_hc.at[j, 3], r_hc.at[j, 3], other)
    for j in range(NJ):
        arrive(far_block(across).at[j], s_hc.at[j, 3], r_hc.at[j, 3])
    multiply(3, across)

    def came_from(i):
        return ((yl + i // NZ) % NYL) * NZ + (z - i % NZ + NZ) % NZ

    for i in range(1, NYL * NZ):
        arrive(landA.at[came_from(i)], s_fa.at[i], r_fa.at[i])
    total = landA[0]
    for i in range(1, NYL * NZ):
        total += landA[i]
    for g, yh_ in ((0, yh), (1, left), (2, right)):
        out_ref[:, pl.ds(pl.multiple_of(yh_ * GW, GW), GW)] = -0.25 * total[:, g * GW : (g + 1) * GW]

    total = sum_x(3)
    for i in range(NYL * NZ):
        shareB[i] = total[i * 4 : i * 4 + 4, :]
    landB[here] = shareB[here]
    for i in range(1, NYL * NZ):
        there = ((yl + i // NZ) % NYL) * NZ + (z + i % NZ) % NZ
        send(shareB.at[there], landB.at[here], s_fb.at[i], r_fb.at[i], yz_peer(i))
    for i in range(1, NYL * NZ):
        arrive(landB.at[came_from(i)], s_fb.at[i], r_fb.at[i])
    total = landB[0]
    for i in range(1, NYL * NZ):
        total += landB[i]
    out_ref[:, pl.ds(pl.multiple_of(across * GW, GW), GW)] = -0.25 * total

    for copy in started:
        copy.wait_send()


def local(three_centre, slot_index, slot_count, panel_last, panel_prev, panel_older):
    slots = slot_index[0, 0]
    key = slots[:, 1] * NBLK + slots[:, 2]
    ids = jnp.arange(SLOTS, dtype=jnp.int32)
    hit = key[None, :] == ids[:, None]
    inv = jnp.sum(jnp.where(hit, ids[None, :], 0), axis=1)
    live = jnp.sum(jnp.where(hit & (ids[None, :] < slot_count[0, 0]), 1, 0), axis=1)

    dma = pltpu.SemaphoreType.DMA
    smem, vmem = pl.BlockSpec(memory_space=pltpu.SMEM), pl.BlockSpec(memory_space=pltpu.VMEM)
    out = pl.pallas_call(
        kernel,
        out_shape=jax.ShapeDtypeStruct((4, NBLK * BLK), F32),
        in_specs=[smem, smem, pl.BlockSpec(memory_space=pl.ANY), vmem, vmem, vmem],
        out_specs=vmem,
        scratch_shapes=[
            pltpu.VMEM((SLOTS, RB, BLK, BLK), BF16),
            pltpu.VMEM((RB, ROWS, NBLK * BLK), BF16),
            pltpu.VMEM((4, OCC), F32),
            pltpu.VMEM((NBAS, 4, OCC), F32),
            pltpu.VMEM((NJ, NRI, 2, 16, LW), BF16),
            pltpu.VMEM((NBAS, NJ, RB, ROWS, LW), BF16),
            pltpu.VMEM((4, ROWS, GW), F32),
            pltpu.VMEM((4, ROWS, GW), BF16),
            pltpu.VMEM((4, NX, XR, GW), BF16),
            pltpu.VMEM((NYL * NZ, 4, 3 * GW), F32),
            pltpu.VMEM((NYL * NZ, 4, GW), F32),
            pltpu.VMEM((NYL * NZ, 4, 3 * GW), F32),
            pltpu.VMEM((NYL * NZ, 4, GW), F32),
            dma,
            dma((NBAS,)), dma((NBAS,)),
            dma((NZ,)), dma((NZ,)),
            dma((NJ, NX * NYL)), dma((NJ, NX * NYL)),
            dma((NJ,)), dma((NJ,)),
            dma((NJ, 4)), dma((NJ, 4)),
            dma((NJ, 4)), dma((NJ, 4)),
            dma((4, NX)), dma((4, NX)),
            dma((NYL * NZ,)), dma((NYL * NZ,)),
            dma((NYL * NZ,)), dma((NYL * NZ,)),
        ],
        compiler_params=pltpu.CompilerParams(
            collective_id=0, has_side_effects=True, vmem_limit_bytes=40 * 1024 * 1024
        ),
        cost_estimate=pl.CostEstimate(flops=2 << 30, bytes_accessed=3 << 20, transcendentals=0),
    )(inv, live, three_centre[0, 0], panel_last, panel_prev, panel_older)
    return out[None, None]


def solution(mesh):
    return jax.shard_map(
        local,
        mesh=mesh,
        in_specs=(
            P("ri", "bas", None, None, None, None),
            P("ri", "bas", None, None),
            P("ri", "bas"),
            P(("ri", "bas"), None),
            P(("ri", "bas"), None),
            P(("ri", "bas"), None),
        ),
        out_specs=P("bas", "ri", None, None),
        check_vma=False,
    )
```

```python
import jax
import jax.numpy as jnp
from jax import lax
from jax.experimental import pallas as pl
from jax.experimental.pallas import tpu as pltpu
from jax.sharding import PartitionSpec as P

MESH = pl.DeviceIdType.MESH
BF16, F32 = jnp.bfloat16, jnp.float32

BLK = 128
NBLK = 16
OCC = 512
RB = 2
SLOTS = 32
ROWS = 256
NX, NYL, NZ, NYH, NC = 4, 2, 8, 4, 2
NRI = NX * NYL * NZ
NBAS = NYH * NC
NJ = 4
LW = OCC // NJ
XR = ROWS // NX
GW = 512


def kernel(
    inv_ref, live_ref, t_hbm, mixed_ref, out_ref,
    t_v, dense, pred, heads, panel, half, part, sent, got, share, land, last, last_got,
    t_sem,
    s_head, r_head, s_z, r_z, s_pair, r_pair, s_line, r_line, s_core, r_core,
    s_y, r_y, s_hc, r_hc, s_x, r_x, s_f, r_f,
):
    ri, bas = lax.axis_index("ri"), lax.axis_index("bas")
    x, yl, z = ri // (NYL * NZ), (ri // NZ) % NYL, ri % NZ
    yh, core = bas // NC, bas % NC
    line = x * NYL + yl
    other = (ri, yh * NC + 1 - core)
    head_core = bas // 4
    head_slot = bas % 4

    def at(x_, yl_, z_):
        return (x_ * NYL + yl_) * NZ + z_

    def head_target(i):
        return (ri, ((yh + i) % NYH) * NC + head_core)

    def z_peer(i):
        return (at(x, yl, (z + i) % NZ), bas)

    def x_peer(i):
        return (at((x + i) % NX, yl, z), bas)

    def xy_peer(i):
        return (at((x + i // NYL) % NX, (yl + i % NYL) % NYL, z), bas)

    def y_peer(i):
        return (ri, ((yh + i) % NYH) * NC + core)

    pair = (at(x, 1 - yl, z), bas)
    started = []

    def remote(src, dst, ssem, rsem, dev):
        return pltpu.make_async_remote_copy(
            src_ref=src, dst_ref=dst, send_sem=ssem, recv_sem=rsem, device_id=dev, device_id_type=MESH
        )

    def send(src, dst, ssem, rsem, dev):
        copy = remote(src, dst, ssem, rsem, dev)
        copy.start()
        started.append(copy)

    def arrive(dst, ssem, rsem):
        remote(dst, dst, ssem, rsem, other).wait_recv()

    t_copy = pltpu.make_async_copy(t_hbm, t_v, t_sem)
    t_copy.start()

    barrier = pltpu.get_barrier_semaphore()

    peers = [(ri, (bas + i) % NBAS) for i in range(1, NBAS)]
    peers += [z_peer(i) for i in range(1, NZ)]
    peers += [xy_peer(i) for i in range(1, NX * NYL)]
    for dev in peers:
        pl.semaphore_signal(barrier, inc=1, device_id=dev, device_id_type=MESH)

    mixed = mixed_ref[...].astype(F32)
    packed = jnp.concatenate([mixed[:, j * LW : (j + 1) * LW] for j in range(NJ)], axis=0).astype(BF16)
    pred[...] = packed
    own_head = core == head_core

    @pl.when(own_head)
    def _():
        heads[head_slot] = packed

    pl.semaphore_wait(barrier, len(peers))

    def head_copy(i):
        return remote(pred, heads.at[head_slot], s_head.at[i], r_head.at[head_slot], head_target(i))

    for i in range(1, NYH):
        copy = head_copy(i)
        copy.start()
        started.append(copy)

    @pl.when(jnp.logical_not(own_head))
    def _():
        head_copy(0).start()

    t_copy.wait()
    for u in range(ROWS // BLK):
        for v in range(NBLK):
            k = u * NBLK + v
            block = t_v[inv_ref[k]]
            block = jnp.where(live_ref[k] != 0, block, jnp.zeros_like(block))
            for p in range(RB):
                dense[pl.ds(p * ROWS + u * BLK, BLK), pl.ds(v * BLK, BLK)] = block[p]

    for k in range(4):
        @pl.when(jnp.logical_not(own_head & (head_slot == k)))
        def _():
            arrive(heads.at[k], s_head.at[0], r_head.at[k])
    rows = [heads[k].astype(F32) for k in range(4)]
    for j in range(NJ):
        tile = jnp.concatenate([r[j * 4 : j * 4 + 4, :] for r in rows], axis=0)
        panel[j, ri, core] = tile.astype(BF16)

    mine = panel.at[:, ri, core]
    for i in range(1, NZ):
        send(mine, mine, s_z.at[i], r_z.at[i], z_peer(i))
    for i in range(1, NZ):
        src = at(x, yl, (z - i + NZ) % NZ)
        arrive(panel.at[:, src, core], s_z.at[i], r_z.at[i])

    def line_of(j, line_):
        return panel.at[j, pl.ds(line_ * NZ, NZ), core]

    pair_line = x * NYL + 1 - yl
    for j in range(NJ):
        mine = line_of(j, line)
        send(mine, mine, s_pair.at[j], r_pair.at[j], pair)

    def pass_own(j):
        mine = line_of(j, line)
        for i in range(1, NX):
            send(mine, mine, s_line.at[j, 0, i], r_line.at[j, 0, i], x_peer(i))

    def pass_pair(j):
        mine = line_of(j, pair_line)
        arrive(mine, s_pair.at[j], r_pair.at[j])
        for i in range(1, NX):
            send(mine, mine, s_line.at[j, 1, i], r_line.at[j, 1, i], x_peer(i))

    left, right = (yh - 1 + NYH) % NYH, (yh + 1) % NYH
    across = (yh + 2) % NYH

    pass_own(0)
    pass_pair(0)
    for j in range(NJ):
        for i in range(1, NX):
            x_ = (x - i + NX) % NX
            arrive(line_of(j, x_ * NYL + yl), s_line.at[j, 0, i], r_line.at[j, 0, i])
            arrive(line_of(j, x_ * NYL + 1 - yl), s_line.at[j, 1, i], r_line.at[j, 1, i])
        if j + 1 < NJ:
            pass_own(j + 1)
            pass_pair(j + 1)
        mine = panel.at[j, :, core]
        send(mine, mine, s_core.at[j], r_core.at[j], other)
        arrive(panel.at[j, :, 1 - core], s_core.at[j], r_core.at[j])
        columns = panel[j].reshape(NBLK * BLK, LW)
        rows = jnp.dot(dense[...], columns, preferred_element_type=F32).astype(BF16)
        for p in range(RB):
            half[bas, j, :, p * LW : (p + 1) * LW] = rows[p * ROWS : (p + 1) * ROWS, :]
        mine = half.at[bas, j]
        send(mine, mine, s_y.at[j, 0], r_y.at[j, 0], y_peer(1))
        send(mine, mine, s_y.at[j, 1], r_y.at[j, 1], y_peer(3))
        send(mine, mine, s_hc.at[j, 0], r_hc.at[j, 0], other)

    def block(yh_):
        return half.at[yh_ * NC + core]

    def far_block(yh_):
        return half.at[yh_ * NC + 1 - core]

    def multiply(g, yh_):
        for c in range(NC):
            total = jnp.zeros((ROWS, ROWS), F32)
            for j in range(NJ):
                total += lax.dot_general(
                    half[bas, j], half[yh_ * NC + c, j], (((1,), (1,)), ((), ())), preferred_element_type=F32
                )
            part[g, :, c * ROWS : (c + 1) * ROWS] = total
            sent[g, :, c * ROWS : (c + 1) * ROWS] = total.astype(BF16)

    def send_x(g):
        for i in range(1, NX):
            x_ = (x + i) % NX
            send(sent.at[g, pl.ds(x_ * XR, XR)], got.at[g, i], s_x.at[g, i], r_x.at[g, i], x_peer(i))

    def fold_x(g):
        for i in range(1, NX):
            arrive(got.at[g, i], s_x.at[g, i], r_x.at[g, i])
        total = part[g, pl.ds(x * XR, XR), :]
        for i in range(1, NX):
            total += got[g, i].astype(F32)
        for z_ in range(NZ):
            for yl_ in range(NYL):
                k = (yl_ * NZ + z_) * 4
                share[g, z_, yl_] = total[k : k + 4, :]
        land[g, z] = share[g, z]
        for i in range(1, NZ):
            send(share.at[g, (z + i) % NZ], land.at[g, z], s_f.at[g, i], r_f.at[g, i], z_peer(i))

    def fold_z(g):
        for i in range(1, NZ):
            arrive(land.at[g, (z - i + NZ) % NZ], s_f.at[g, i], r_f.at[g, i])
        for yl_ in range(NYL):
            total = land[g, 0, yl_]
            for z_ in range(1, NZ):
                total += land[g, z_, yl_]
            last[g, yl_] = total
        send(last.at[g, 1 - yl], last_got.at[g], s_f.at[g, 0], r_f.at[g, 0], pair)

    def finish(g, yh_):
        arrive(last_got.at[g], s_f.at[g, 0], r_f.at[g, 0])
        out_ref[:, pl.ds(pl.multiple_of(yh_ * GW, GW), GW)] = -0.25 * (last[g, yl] + last_got[g])

    for j in range(NJ):
        arrive(far_block(yh).at[j], s_hc.at[j, 0], r_hc.at[j, 0])
    multiply(0, yh)
    send_x(0)

    def forward(j):
        if j % 2 == 0:
            mine = block(left).at[j]
            send(mine, mine, s_y.at[j, 2], r_y.at[j, 2], y_peer(1))
        else:
            mine = block(right).at[j]
            send(mine, mine, s_y.at[j, 2], r_y.at[j, 2], y_peer(3))

    for j in range(NJ):
        mine = block(left).at[j]
        arrive(mine, s_y.at[j, 0], r_y.at[j, 0])
        send(mine, mine, s_hc.at[j, 1], r_hc.at[j, 1], other)
        mine = block(right).at[j]
        arrive(mine, s_y.at[j, 1], r_y.at[j, 1])
        send(mine, mine, s_hc.at[j, 2], r_hc.at[j, 2], other)
        if j == 0:
            fold_x(0)
        if j == NJ - 2:
            forward(0)
            forward(1)
    for j in range(2, NJ):
        forward(j)
    for g, yh_ in ((1, left), (2, right)):
        for j in range(NJ):
            arrive(far_block(yh_).at[j], s_hc.at[j, g], r_hc.at[j, g])
        multiply(g, yh_)
        send_x(g)
    fold_x(1)
    fold_x(2)

    for j in range(NJ):
        mine = block(across).at[j]
        arrive(mine, s_y.at[j, 2], r_y.at[j, 2])
        send(mine, mine, s_hc.at[j, 3], r_hc.at[j, 3], other)
    for j in range(NJ):
        arrive(far_block(across).at[j], s_hc.at[j, 3], r_hc.at[j, 3])
    multiply(3, across)

    for i in range(1, NX * NYL):
        line_ = ((x + i // NYL) % NX) * NYL + (yl + i % NYL) % NYL
        src = sent.at[3, pl.ds(line_ * 32, 32)]
        dst = got.at[3, i // NYL, pl.ds((i % NYL) * 32, 32)]
        send(src, dst, s_f.at[3, i], r_f.at[3, i], xy_peer(i))
    for g in range(3):
        fold_z(g)
    for i in range(1, NX * NYL):
        arrive(got.at[3, i // NYL, pl.ds((i % NYL) * 32, 32)], s_f.at[3, i], r_f.at[3, i])
    total = part[3, pl.ds(line * 32, 32), :]
    for i in range(1, NX * NYL):
        total += got[3, i // NYL, (i % NYL) * 32 : (i % NYL) * 32 + 32, :].astype(F32)
    for i in range(NZ):
        share[3, i, 0] = total[i * 4 : i * 4 + 4, :]
    land[3, z, 0] = share[3, z, 0]
    for i in range(1, NZ):
        src, dst = share.at[3, (z + i) % NZ, 0], land.at[3, z, 0]
        send(src, dst, s_f.at[3, NX * NYL + i], r_f.at[3, NX * NYL + i], z_peer(i))
    finish(0, yh)
    finish(1, left)
    finish(2, right)
    for i in range(1, NZ):
        arrive(land.at[3, (z - i + NZ) % NZ, 0], s_f.at[3, NX * NYL + i], r_f.at[3, NX * NYL + i])
    total = land[3, 0, 0]
    for i in range(1, NZ):
        total += land[3, i, 0]
    out_ref[:, pl.ds(pl.multiple_of(across * GW, GW), GW)] = -0.25 * total

    for copy in started:
        copy.wait_send()

    @pl.when(jnp.logical_not(own_head))
    def _():
        head_copy(0).wait_send()


def local(three_centre, slot_index, slot_count, panel_last, panel_prev, panel_older):
    mixed = (
        2.5 * panel_last.astype(F32) - 2.0 * panel_prev.astype(F32) + 0.5 * panel_older.astype(F32)
    ).astype(BF16)
    slots = slot_index[0, 0]
    key = slots[:, 1] * NBLK + slots[:, 2]
    ids = jnp.arange(SLOTS, dtype=jnp.int32)
    hit = key[None, :] == ids[:, None]
    inv = jnp.sum(jnp.where(hit, ids[None, :], 0), axis=1)
    live = jnp.sum(jnp.where(hit & (ids[None, :] < slot_count[0, 0]), 1, 0), axis=1)

    dma = pltpu.SemaphoreType.DMA
    smem, vmem = pl.BlockSpec(memory_space=pltpu.SMEM), pl.BlockSpec(memory_space=pltpu.VMEM)
    out = pl.pallas_call(
        kernel,
        out_shape=jax.ShapeDtypeStruct((4, NBLK * BLK), F32),
        in_specs=[smem, smem, pl.BlockSpec(memory_space=pl.ANY), vmem],
        out_specs=vmem,
        scratch_shapes=[
            pltpu.VMEM((SLOTS, RB, BLK, BLK), BF16),
            pltpu.VMEM((RB * ROWS, NBLK * BLK), BF16),
            pltpu.VMEM((16, BLK), BF16),
            pltpu.VMEM((4, 16, BLK), BF16),
            pltpu.VMEM((NJ, NRI, 2, 16, LW), BF16),
            pltpu.VMEM((NBAS, NJ, ROWS, RB * LW), BF16),
            pltpu.VMEM((4, ROWS, GW), F32),
            pltpu.VMEM((4, ROWS, GW), BF16),
            pltpu.VMEM((4, NX, XR, GW), BF16),
            pltpu.VMEM((4, NZ, NYL, 4, GW), F32),
            pltpu.VMEM((4, NZ, NYL, 4, GW), F32),
            pltpu.VMEM((3, NYL, 4, GW), F32),
            pltpu.VMEM((3, 4, GW), F32),
            dma,
            dma((NYH,)), dma((4,)),
            dma((NZ,)), dma((NZ,)),
            dma((NJ,)), dma((NJ,)),
            dma((NJ, NYL, NX)), dma((NJ, NYL, NX)),
            dma((NJ,)), dma((NJ,)),
            dma((NJ, 3)), dma((NJ, 3)),
            dma((NJ, 4)), dma((NJ, 4)),
            dma((3, NX)), dma((3, NX)),
            dma((4, NYL * NZ)), dma((4, NYL * NZ)),
        ],
        compiler_params=pltpu.CompilerParams(
            collective_id=0, has_side_effects=True, vmem_limit_bytes=53 * 1024 * 1024
        ),
        cost_estimate=pl.CostEstimate(flops=2 << 30, bytes_accessed=3 << 20, transcendentals=0),
    )(inv, live, three_centre[0, 0], mixed)
    return out[None, None]


def solution(mesh):
    return jax.shard_map(
        local,
        mesh=mesh,
        in_specs=(
            P("ri", "bas", None, None, None, None),
            P("ri", "bas", None, None),
            P("ri", "bas"),
            P(("ri", "bas"), None),
            P(("ri", "bas"), None),
            P(("ri", "bas"), None),
        ),
        out_specs=P("bas", "ri", None, None),
        check_vma=False,
    )
```

```python
import jax
import jax.numpy as jnp
from jax import lax
from jax.experimental import pallas as pl
from jax.experimental.pallas import tpu as pltpu
from jax.sharding import PartitionSpec as P

MESH = pl.DeviceIdType.MESH
BF16, F32 = jnp.bfloat16, jnp.float32

BLK = 128
NBLK = 16
OCC = 512
RB = 2
SLOTS = 32
ROWS = 256
NX, NYL, NZ, NYH, NC = 4, 2, 8, 4, 2
NRI = NX * NYL * NZ
NBAS = NYH * NC
NJ = 4
LW = OCC // NJ
XR = ROWS // NX
GW = 512


def kernel(
    t_hbm, slots_hbm, count_hbm, last_hbm, prev_hbm, older_hbm, out_ref,
    t_v, slots_v, count_v, panels_v, table_v, table, dense, pred, heads, panel, half, part, sent, got, share, land, last, last_got,
    in_sem,
    s_head, r_head, s_z, r_z, s_xy, r_xy, s_lc, r_lc, s_pair, r_pair, s_line, r_line, s_core, r_core,
    s_y, r_y, s_hc, r_hc, s_x, r_x, s_f, r_f, s_last, r_last,
):
    ri, bas = lax.axis_index("ri"), lax.axis_index("bas")
    x, yl, z = ri // (NYL * NZ), (ri // NZ) % NYL, ri % NZ
    yh, core = bas // NC, bas % NC
    line = x * NYL + yl
    other = (ri, yh * NC + 1 - core)
    head_core = bas // 4
    head_slot = bas % 4

    def at(x_, yl_, z_):
        return (x_ * NYL + yl_) * NZ + z_

    def head_target(i):
        return (ri, ((yh + i) % NYH) * NC + head_core)

    def z_peer(i):
        return (at(x, yl, (z + i) % NZ), bas)

    def x_peer(i):
        return (at((x + i) % NX, yl, z), bas)

    def xy_peer(i):
        return (at((x + i // NYL) % NX, (yl + i % NYL) % NYL, z), bas)

    def y_peer(i):
        return (ri, ((yh + i) % NYH) * NC + core)

    pair = (at(x, 1 - yl, z), bas)
    started = []

    def remote(src, dst, ssem, rsem, dev):
        return pltpu.make_async_remote_copy(
            src_ref=src, dst_ref=dst, send_sem=ssem, recv_sem=rsem, device_id=dev, device_id_type=MESH
        )

    def send(src, dst, ssem, rsem, dev):
        copy = remote(src, dst, ssem, rsem, dev)
        copy.start()
        started.append(copy)

    def arrive(dst, ssem, rsem):
        remote(dst, dst, ssem, rsem, other).wait_recv()

    loads = [
        pltpu.make_async_copy(src, dst, in_sem.at[i])
        for i, (src, dst) in enumerate((
            (last_hbm, panels_v.at[0]), (prev_hbm, panels_v.at[1]), (older_hbm, panels_v.at[2]),
            (slots_hbm, slots_v), (count_hbm, count_v), (t_hbm, t_v),
        ))
    ]
    for copy in loads:
        copy.start()

    barrier = pltpu.get_barrier_semaphore()

    peers = [(ri, (bas + i) % NBAS) for i in range(1, NBAS)]
    peers += [z_peer(i) for i in range(1, NZ)]
    peers += [xy_peer(i) for i in range(1, NX * NYL)]
    for dev in peers:
        pl.semaphore_signal(barrier, inc=1, device_id=dev, device_id_type=MESH)

    for copy in loads[:3]:
        copy.wait()
    panels = [panels_v[i].astype(F32) for i in range(3)]
    mixed = 2.5 * panels[0] - 2.0 * panels[1] + 0.5 * panels[2]
    packed = jnp.concatenate([mixed[:, j * LW : (j + 1) * LW] for j in range(NJ)], axis=0).astype(BF16)
    pred[...] = packed
    own_head = core == head_core

    @pl.when(own_head)
    def _():
        heads[head_slot] = packed

    pl.semaphore_wait(barrier, len(peers))

    def head_copy(i):
        return remote(pred, heads.at[head_slot], s_head.at[i], r_head.at[head_slot], head_target(i))

    for i in range(1, NYH):
        copy = head_copy(i)
        copy.start()
        started.append(copy)

    @pl.when(jnp.logical_not(own_head))
    def _():
        head_copy(0).start()

    loads[3].wait()
    loads[4].wait()
    key = slots_v[0, 1] * NBLK + slots_v[0, 2]
    slot = lax.broadcasted_iota(jnp.int32, (SLOTS, SLOTS), 1)
    hit = lax.broadcasted_iota(jnp.int32, (SLOTS, SLOTS), 0) == key
    used = hit & (slot < count_v[...])
    inv = jnp.max(jnp.where(hit, slot, 0), axis=1, keepdims=True)
    live = jnp.sum(jnp.where(used, 1, 0), axis=1, keepdims=True)
    table_v[0] = jnp.broadcast_to(inv, (SLOTS, BLK))
    table_v[1] = jnp.broadcast_to(live, (SLOTS, BLK))
    copy = pltpu.make_async_copy(table_v, table, in_sem.at[6])
    copy.start()
    copy.wait()
    loads[5].wait()
    for u in range(ROWS // BLK):
        for v in range(NBLK):
            k = u * NBLK + v
            block = t_v[table[0, k, 0]]
            block = jnp.where(table[1, k, 0] != 0, block, jnp.zeros_like(block))
            for p in range(RB):
                dense[pl.ds(p * ROWS + u * BLK, BLK), pl.ds(v * BLK, BLK)] = block[p]

    for k in range(4):
        @pl.when(jnp.logical_not(own_head & (head_slot == k)))
        def _():
            arrive(heads.at[k], s_head.at[0], r_head.at[k])
    rows = [heads[k].astype(F32) for k in range(4)]
    for j in range(NJ):
        tile = jnp.concatenate([r[j * 4 : j * 4 + 4, :] for r in rows], axis=0)
        panel[j, ri, core] = tile.astype(BF16)

    mine = panel.at[:, ri, core]
    for i in range(1, NZ):
        send(mine, mine, s_z.at[i], r_z.at[i], z_peer(i))
    for i in range(1, NZ):
        src = at(x, yl, (z - i + NZ) % NZ)
        arrive(panel.at[:, src, core], s_z.at[i], r_z.at[i])

    def line_of(j, line_):
        return panel.at[j, pl.ds(line_ * NZ, NZ), core]

    pair_line = x * NYL + 1 - yl
    def pass_core(line_):
        mine = line_of(0, line_)
        send(mine, mine, s_lc.at[line_], r_lc.at[line_], other)

    mine = line_of(0, line)
    for i in range(1, NX * NYL):
        send(mine, mine, s_xy.at[i], r_xy.at[i], xy_peer(i))
    pass_core(line)
    for j in range(1, NJ):
        mine = line_of(j, line)
        send(mine, mine, s_pair.at[j], r_pair.at[j], pair)

    def pass_own(j):
        mine = line_of(j, line)
        for i in range(1, NX):
            send(mine, mine, s_line.at[j, 0, i], r_line.at[j, 0, i], x_peer(i))

    def pass_pair(j):
        mine = line_of(j, pair_line)
        arrive(mine, s_pair.at[j], r_pair.at[j])
        for i in range(1, NX):
            send(mine, mine, s_line.at[j, 1, i], r_line.at[j, 1, i], x_peer(i))

    left, right = (yh - 1 + NYH) % NYH, (yh + 1) % NYH
    across = (yh + 2) % NYH

    for j in range(NJ):
        if j == 0:
            for i in (1, 2, 6, 3, 7, 4, 5):
                line_ = ((x - i // NYL + NX) % NX) * NYL + (yl + i % NYL) % NYL
                arrive(line_of(0, line_), s_xy.at[i], r_xy.at[i])
                pass_core(line_)
                if i == 6:
                    pass_own(1)
            pass_pair(1)
        else:
            for i in range(1, NX):
                x_ = (x - i + NX) % NX
                arrive(line_of(j, x_ * NYL + yl), s_line.at[j, 0, i], r_line.at[j, 0, i])
                arrive(line_of(j, x_ * NYL + 1 - yl), s_line.at[j, 1, i], r_line.at[j, 1, i])
        if j == 0:
            for line_ in range(NX * NYL):
                arrive(panel.at[0, pl.ds(line_ * NZ, NZ), 1 - core], s_lc.at[line_], r_lc.at[line_])
        else:
            mine = panel.at[j, :, core]
            send(mine, mine, s_core.at[j], r_core.at[j], other)
            arrive(panel.at[j, :, 1 - core], s_core.at[j], r_core.at[j])
        columns = panel[j].reshape(NBLK * BLK, LW)
        rows = jnp.dot(dense[...], columns, preferred_element_type=F32).astype(BF16)
        for p in range(RB):
            half[bas, j, :, p * LW : (p + 1) * LW] = rows[p * ROWS : (p + 1) * ROWS, :]
        mine = half.at[bas, j]
        send(mine, mine, s_y.at[j, 0], r_y.at[j, 0], y_peer(1))
        send(mine, mine, s_y.at[j, 1], r_y.at[j, 1], y_peer(3))
        send(mine, mine, s_hc.at[j, 0], r_hc.at[j, 0], other)
        if j + 2 < NJ:
            pass_own(j + 2)
            pass_pair(j + 2)

    def block(yh_):
        return half.at[yh_ * NC + core]

    def far_block(yh_):
        return half.at[yh_ * NC + 1 - core]

    def multiply(g, yh_, c, chunks, first=True, last=True):
        cols = pl.ds(pl.multiple_of(c * ROWS, ROWS), ROWS)
        total = jnp.zeros((ROWS, ROWS), F32) if first else part[g, :, cols]
        for j in chunks:
            total += lax.dot_general(
                half[bas, j], half[yh_ * NC + c, j], (((1,), (1,)), ((), ())), preferred_element_type=F32
            )
        part[g, :, cols] = total
        if last:
            sent[g, :, cols] = total.astype(BF16)

    def send_x(g):
        for i in range(1, NX):
            x_ = (x + i) % NX
            send(sent.at[g, pl.ds(x_ * XR, XR)], got.at[g, i], s_x.at[g, i], r_x.at[g, i], x_peer(i))

    def fold_x(g):
        for i in range(1, NX):
            arrive(got.at[g, i], s_x.at[g, i], r_x.at[g, i])
        total = part[g, pl.ds(x * XR, XR), :]
        for i in range(1, NX):
            total += got[g, i].astype(F32)
        for z_ in range(NZ):
            for yl_ in range(NYL):
                k = (yl_ * NZ + z_) * 4
                share[g, z_, yl_] = total[k : k + 4, :]
        land[g, z] = share[g, z]
        for i in range(1, NZ):
            send(share.at[g, (z + i) % NZ], land.at[g, z], s_f.at[g, i], r_f.at[g, i], z_peer(i))

    def fold_z(g):
        for i in range(1, NZ):
            arrive(land.at[g, (z - i + NZ) % NZ], s_f.at[g, i], r_f.at[g, i])
        for yl_ in range(NYL):
            total = land[g, 0, yl_]
            for z_ in range(1, NZ):
                total += land[g, z_, yl_]
            last[g, yl_] = total
        send(last.at[g, 1 - yl], last_got.at[g], s_f.at[g, 0], r_f.at[g, 0], pair)

    def finish(g, yh_):
        arrive(last_got.at[g], s_f.at[g, 0], r_f.at[g, 0])
        out_ref[:, pl.ds(pl.multiple_of(yh_ * GW, GW), GW)] = -0.25 * (last[g, yl] + last_got[g])

    for j in range(NJ):
        arrive(far_block(yh).at[j], s_hc.at[j, 0], r_hc.at[j, 0])
    for c in range(NC):
        multiply(0, yh, c, range(NJ))
    send_x(0)

    def forward(j):
        if j % 2 == 0:
            mine = block(left).at[j]
            send(mine, mine, s_y.at[j, 2], r_y.at[j, 2], y_peer(1))
        else:
            mine = block(right).at[j]
            send(mine, mine, s_y.at[j, 2], r_y.at[j, 2], y_peer(3))

    for j in range(NJ):
        mine = block(left).at[j]
        arrive(mine, s_y.at[j, 0], r_y.at[j, 0])
        send(mine, mine, s_hc.at[j, 1], r_hc.at[j, 1], other)
        mine = block(right).at[j]
        arrive(mine, s_y.at[j, 1], r_y.at[j, 1])
        send(mine, mine, s_hc.at[j, 2], r_hc.at[j, 2], other)
        if j == 0:
            fold_x(0)
        if j == NJ - 2:
            forward(0)
            forward(1)
    for j in range(2, NJ):
        forward(j)
    for g, yh_ in ((1, left), (2, right)):
        for j in range(NJ):
            arrive(far_block(yh_).at[j], s_hc.at[j, g], r_hc.at[j, g])
        for c in range(NC):
            multiply(g, yh_, c, range(NJ))
        send_x(g)
    def far(chunks):
        for j in chunks:
            mine = block(across).at[j]
            arrive(mine, s_y.at[j, 2], r_y.at[j, 2])
            send(mine, mine, s_hc.at[j, 3], r_hc.at[j, 3], other)

    def far_other(chunks):
        for j in chunks:
            arrive(far_block(across).at[j], s_hc.at[j, 3], r_hc.at[j, 3])

    def last_parts(i, c):
        cols = pl.ds(pl.multiple_of(c * ROWS, ROWS), ROWS)
        return got.at[3, i // NYL, pl.ds((i % NYL) * 32, 32), cols], cols

    def send_last(k, c):
        for i in range(1, NX * NYL):
            line_ = ((x + i // NYL) % NX) * NYL + (yl + i % NYL) % NYL
            dst, cols = last_parts(i, c)
            send(sent.at[3, pl.ds(line_ * 32, 32), cols], dst, s_last.at[k, i], r_last.at[k, i], xy_peer(i))

    far((0, 1))
    fold_x(1)
    far_other((0, 1))
    for c in range(NC):
        multiply(3, across, c, (0, 1), True, False)
    fold_x(2)
    far((2, 3))
    multiply(3, across, core, (2, 3), False, True)
    send_last(0, core)
    far_other((2, 3))
    multiply(3, across, 1 - core, (2, 3), False, True)
    send_last(1, 1 - core)
    for g in range(3):
        fold_z(g)
    for k, c in ((0, core), (1, 1 - core)):
        for i in range(1, NX * NYL):
            arrive(last_parts(i, c)[0], s_last.at[k, i], r_last.at[k, i])
    total = part[3, pl.ds(line * 32, 32), :]
    for i in range(1, NX * NYL):
        total += got[3, i // NYL, (i % NYL) * 32 : (i % NYL) * 32 + 32, :].astype(F32)
    for i in range(NZ):
        share[3, i, 0] = total[i * 4 : i * 4 + 4, :]
    land[3, z, 0] = share[3, z, 0]
    for i in range(1, NZ):
        src, dst = share.at[3, (z + i) % NZ, 0], land.at[3, z, 0]
        send(src, dst, s_f.at[3, i], r_f.at[3, i], z_peer(i))
    finish(0, yh)
    finish(1, left)
    finish(2, right)
    for i in range(1, NZ):
        arrive(land.at[3, (z - i + NZ) % NZ, 0], s_f.at[3, i], r_f.at[3, i])
    total = land[3, 0, 0]
    for i in range(1, NZ):
        total += land[3, i, 0]
    out_ref[:, pl.ds(pl.multiple_of(across * GW, GW), GW)] = -0.25 * total

    for copy in started:
        copy.wait_send()

    @pl.when(jnp.logical_not(own_head))
    def _():
        head_copy(0).wait_send()


def local(three_centre, slot_index, slot_count, panel_last, panel_prev, panel_older):
    slots = jnp.transpose(slot_index, (0, 3, 1, 2))
    dma = pltpu.SemaphoreType.DMA
    hbm, vmem = pl.BlockSpec(memory_space=pltpu.HBM), pl.BlockSpec(memory_space=pltpu.VMEM)
    out = pl.pallas_call(
        kernel,
        out_shape=jax.ShapeDtypeStruct((4, NBLK * BLK), F32),
        in_specs=[hbm] * 6,
        out_specs=vmem,
        scratch_shapes=[
            pltpu.VMEM((SLOTS, RB, BLK, BLK), BF16),
            pltpu.VMEM((1, 3, 1, SLOTS), jnp.int32),
            pltpu.VMEM((1, 1), jnp.int32),
            pltpu.VMEM((3, 4, OCC), BF16),
            pltpu.VMEM((2, SLOTS, BLK), jnp.int32),
            pltpu.SMEM((2, SLOTS, BLK), jnp.int32),
            pltpu.VMEM((RB * ROWS, NBLK * BLK), BF16),
            pltpu.VMEM((16, BLK), BF16),
            pltpu.VMEM((4, 16, BLK), BF16),
            pltpu.VMEM((NJ, NRI, 2, 16, LW), BF16),
            pltpu.VMEM((NBAS, NJ, ROWS, RB * LW), BF16),
            pltpu.VMEM((4, ROWS, GW), F32),
            pltpu.VMEM((4, ROWS, GW), BF16),
            pltpu.VMEM((4, NX, XR, GW), BF16),
            pltpu.VMEM((4, NZ, NYL, 4, GW), F32),
            pltpu.VMEM((4, NZ, NYL, 4, GW), F32),
            pltpu.VMEM((3, NYL, 4, GW), F32),
            pltpu.VMEM((3, 4, GW), F32),
            dma((7,)),
            dma((NYH,)), dma((4,)),
            dma((NZ,)), dma((NZ,)),
            dma((NX * NYL,)), dma((NX * NYL,)),
            dma((NX * NYL,)), dma((NX * NYL,)),
            dma((NJ,)), dma((NJ,)),
            dma((NJ, NYL, NX)), dma((NJ, NYL, NX)),
            dma((NJ,)), dma((NJ,)),
            dma((NJ, 3)), dma((NJ, 3)),
            dma((NJ, 4)), dma((NJ, 4)),
            dma((3, NX)), dma((3, NX)),
            dma((4, NZ)), dma((4, NZ)),
            dma((NC, NX * NYL)), dma((NC, NX * NYL)),
        ],
        compiler_params=pltpu.CompilerParams(
            collective_id=0, has_side_effects=True, vmem_limit_bytes=60 * 1024 * 1024
        ),
        cost_estimate=pl.CostEstimate(flops=2 << 30, bytes_accessed=3 << 20, transcendentals=0),
    )(three_centre[0, 0], slots, slot_count, panel_last, panel_prev, panel_older)
    return out[None, None]


def solution(mesh):
    return jax.shard_map(
        local,
        mesh=mesh,
        in_specs=(
            P("ri", "bas", None, None, None, None),
            P("ri", "bas", None, None),
            P("ri", "bas"),
            P(("ri", "bas"), None),
            P(("ri", "bas"), None),
            P(("ri", "bas"), None),
        ),
        out_specs=P("bas", "ri", None, None),
        check_vma=False,
    )
```

```python
import jax
import jax.numpy as jnp
from jax import lax
from jax.experimental import pallas as pl
from jax.experimental.pallas import tpu as pltpu
from jax.sharding import PartitionSpec as P

MESH = pl.DeviceIdType.MESH
BF16, F32 = jnp.bfloat16, jnp.float32

BLK = 128
NBLK = 16
OCC = 512
RB = 2
SLOTS = 32
ROWS = 256
NX, NYL, NZ, NYH, NC = 4, 2, 8, 4, 2
NRI = NX * NYL * NZ
NBAS = NYH * NC
NJ = 4
LW = OCC // NJ
XR = ROWS // NX
GW = 512


def kernel(
    t_hbm, slots_hbm, count_hbm, last_hbm, prev_hbm, older_hbm, out_ref,
    t_v, slots_v, count_v, panels_v, table_v, table, dense, pred, heads, panel, half, near, far,
    part, sent, got, share, land, last, fin,
    in_sem,
    s_head, r_head, s_z, r_z, s_xy, r_xy, s_lc, r_lc, s_pair, r_pair, s_line, r_line, s_core, r_core,
    s_y, r_y, s_hc, r_hc, s_x, r_x, s_f, r_f, s_fin, r_fin,
):
    ri, bas = lax.axis_index("ri"), lax.axis_index("bas")
    x, yl, z = ri // (NYL * NZ), (ri // NZ) % NYL, ri % NZ
    yh, core = bas // NC, bas % NC
    line = x * NYL + yl
    other = (ri, yh * NC + 1 - core)
    head_core = bas // 4
    head_slot = bas % 4

    def at(x_, yl_, z_):
        return (x_ * NYL + yl_) * NZ + z_

    def head_target(i):
        return (ri, ((yh + i) % NYH) * NC + head_core)

    def z_peer(i):
        return (at(x, yl, (z + i) % NZ), bas)

    def x_peer(i):
        return (at((x + i) % NX, yl, z), bas)

    def xy_peer(i):
        return (at((x + i // NYL) % NX, (yl + i % NYL) % NYL, z), bas)

    y = yh * NYL + yl

    def y_chip(d):
        y_ = (y + d + NYL * NYH) % (NYL * NYH)
        return (at(x, y_ % NYL, z), (y_ // NYL) * NC + core)

    pair = (at(x, 1 - yl, z), bas)
    started = []

    def remote(src, dst, ssem, rsem, dev):
        return pltpu.make_async_remote_copy(
            src_ref=src, dst_ref=dst, send_sem=ssem, recv_sem=rsem, device_id=dev, device_id_type=MESH
        )

    def send(src, dst, ssem, rsem, dev):
        copy = remote(src, dst, ssem, rsem, dev)
        copy.start()
        started.append(copy)

    def drain(keep=0):
        while len(started) > keep:
            started.pop(0).wait_send()

    def arrive(dst, ssem, rsem):
        remote(dst, dst, ssem, rsem, other).wait_recv()

    loads = [
        pltpu.make_async_copy(src, dst, in_sem.at[i])
        for i, (src, dst) in enumerate((
            (last_hbm, panels_v.at[0]), (prev_hbm, panels_v.at[1]), (older_hbm, panels_v.at[2]),
            (slots_hbm, slots_v), (count_hbm, count_v), (t_hbm, t_v),
        ))
    ]
    for copy in loads:
        copy.start()

    barrier = pltpu.get_barrier_semaphore()

    peers = [(ri, (bas + i) % NBAS) for i in range(1, NBAS)]
    peers += [z_peer(i) for i in range(1, NZ)]
    peers += [xy_peer(i) for i in range(1, NX * NYL)]
    peers += [(at(x, 1 - yl, z), ((yh + i) % NYH) * NC + core) for i in (1, 3)]
    for dev in peers:
        pl.semaphore_signal(barrier, inc=1, device_id=dev, device_id_type=MESH)

    for copy in loads[:3]:
        copy.wait()
    panels = [panels_v[i].astype(F32) for i in range(3)]
    mixed = 2.5 * panels[0] - 2.0 * panels[1] + 0.5 * panels[2]
    packed = jnp.concatenate([mixed[:, j * LW : (j + 1) * LW] for j in range(NJ)], axis=0).astype(BF16)
    pred[...] = packed
    own_head = core == head_core

    @pl.when(own_head)
    def _():
        heads[head_slot] = packed

    pl.semaphore_wait(barrier, len(peers))

    def head_copy(i):
        return remote(pred, heads.at[head_slot], s_head.at[i], r_head.at[head_slot], head_target(i))

    for i in range(1, NYH):
        copy = head_copy(i)
        copy.start()
        started.append(copy)

    @pl.when(jnp.logical_not(own_head))
    def _():
        head_copy(0).start()

    loads[3].wait()
    loads[4].wait()
    key = slots_v[0, 1] * NBLK + slots_v[0, 2]
    slot = lax.broadcasted_iota(jnp.int32, (SLOTS, SLOTS), 1)
    hit = lax.broadcasted_iota(jnp.int32, (SLOTS, SLOTS), 0) == key
    used = hit & (slot < count_v[...])
    inv = jnp.max(jnp.where(hit, slot, 0), axis=1, keepdims=True)
    live = jnp.sum(jnp.where(used, 1, 0), axis=1, keepdims=True)
    table_v[0] = jnp.broadcast_to(inv, (SLOTS, BLK))
    table_v[1] = jnp.broadcast_to(live, (SLOTS, BLK))
    copy = pltpu.make_async_copy(table_v, table, in_sem.at[6])
    copy.start()
    copy.wait()
    loads[5].wait()
    for u in range(ROWS // BLK):
        for v in range(NBLK):
            k = u * NBLK + v
            block = t_v[table[0, k, 0]]
            block = jnp.where(table[1, k, 0] != 0, block, jnp.zeros_like(block))
            for p in range(RB):
                dense[pl.ds(p * ROWS + u * BLK, BLK), pl.ds(v * BLK, BLK)] = block[p]

    for k in range(4):
        @pl.when(jnp.logical_not(own_head & (head_slot == k)))
        def _():
            arrive(heads.at[k], s_head.at[0], r_head.at[k])
    rows = [heads[k].astype(F32) for k in range(4)]
    for j in range(NJ):
        tile = jnp.concatenate([r[j * 4 : j * 4 + 4, :] for r in rows], axis=0)
        panel[j, ri, core] = tile.astype(BF16)

    parts = (pl.ds(0, 1), pl.ds(1, NJ - 1))
    for k, part_ in enumerate(parts):
        mine = panel.at[part_, ri, core]
        for i in range(1, NZ):
            send(mine, mine, s_z.at[k, i], r_z.at[k, i], z_peer(i))

    def arrive_z(k):
        for i in range(1, NZ):
            src = at(x, yl, (z - i + NZ) % NZ)
            arrive(panel.at[parts[k], src, core], s_z.at[k, i], r_z.at[k, i])

    arrive_z(0)

    def line_of(j, line_):
        return panel.at[j, pl.ds(line_ * NZ, NZ), core]

    pair_line = x * NYL + 1 - yl
    def pass_core(line_):
        mine = line_of(0, line_)
        send(mine, mine, s_lc.at[line_], r_lc.at[line_], other)

    mine = line_of(0, line)
    for i in range(1, NX * NYL):
        send(mine, mine, s_xy.at[i], r_xy.at[i], xy_peer(i))
    pass_core(line)
    arrive_z(1)
    for j in range(1, NJ):
        mine = line_of(j, line)
        send(mine, mine, s_pair.at[j], r_pair.at[j], pair)

    def pass_own(j):
        mine = line_of(j, line)
        for i in range(1, NX):
            send(mine, mine, s_line.at[j, 0, i], r_line.at[j, 0, i], x_peer(i))

    def pass_pair(j):
        mine = line_of(j, pair_line)
        arrive(mine, s_pair.at[j], r_pair.at[j])
        for i in range(1, NX):
            send(mine, mine, s_line.at[j, 1, i], r_line.at[j, 1, i], x_peer(i))

    before, after = (yh - 1 + NYH) % NYH, (yh + 1) % NYH
    across = (yh + 2) % NYH

    def pass_near(j):
        for s in range(2):
            mine = near.at[s, core, j]
            arrive(mine, s_y.at[j, s], r_y.at[j, s])
            d = 1 - 2 * s
            p = ((y + d + NYL * NYH) % (NYL * NYH)) // 4
            send(near.at[s, core, j, p], far.at[s, core, j], s_y.at[j, 2 + s], r_y.at[j, 2 + s], y_chip(d))
            send(mine, mine, s_hc.at[j, 1 + s], r_hc.at[j, 1 + s], other)

    for j in range(NJ):
        if j == 0:
            for i in (1, 2, 6, 3, 7, 4, 5):
                line_ = ((x - i // NYL + NX) % NX) * NYL + (yl + i % NYL) % NYL
                arrive(line_of(0, line_), s_xy.at[i], r_xy.at[i])
                pass_core(line_)
                if i == 6:
                    pass_own(1)
            pass_pair(1)
        else:
            for i in range(1, NX):
                x_ = (x - i + NX) % NX
                arrive(line_of(j, x_ * NYL + yl), s_line.at[j, 0, i], r_line.at[j, 0, i])
                arrive(line_of(j, x_ * NYL + 1 - yl), s_line.at[j, 1, i], r_line.at[j, 1, i])
        if j == 0:
            for line_ in range(NX * NYL):
                arrive(panel.at[0, pl.ds(line_ * NZ, NZ), 1 - core], s_lc.at[line_], r_lc.at[line_])
        else:
            mine = panel.at[j, :, core]
            send(mine, mine, s_core.at[j], r_core.at[j], other)
            arrive(panel.at[j, :, 1 - core], s_core.at[j], r_core.at[j])
        columns = panel[j].reshape(NBLK * BLK, LW)
        rows = jnp.dot(dense[...], columns, preferred_element_type=F32).astype(BF16)
        for p in range(RB):
            half[core, j, p] = rows[p * ROWS : (p + 1) * ROWS, :]
        mine = half.at[core, j]
        send(mine, near.at[0, core, j], s_y.at[j, 0], r_y.at[j, 0], y_chip(1))
        send(mine, near.at[1, core, j], s_y.at[j, 1], r_y.at[j, 1], y_chip(-1))
        send(mine, mine, s_hc.at[j, 0], r_hc.at[j, 0], other)
        if j + 2 < NJ:
            pass_own(j + 2)
            pass_pair(j + 2)
        if j >= 2:
            pass_near(j - 2)

    same, away = 1 - yl, yl
    away_yh = jnp.where(yl == 1, after, before)

    def wide(ref, *at_):
        return jnp.concatenate([ref[(*at_, p)] for p in range(RB)], axis=1)

    def multiply(g, rows, columns):
        for c in range(NC):
            total = jnp.zeros((ROWS, ROWS), F32)
            for lhs, rhs in zip(rows, columns(c), strict=True):
                total += lax.dot_general(lhs, rhs, (((1,), (1,)), ((), ())), preferred_element_type=F32)
            part[g, :, c * ROWS : (c + 1) * ROWS] = total
            sent[g, :, c * ROWS : (c + 1) * ROWS] = total.astype(BF16)
        for i in range(1, NX):
            x_ = (x + i) % NX
            send(sent.at[g, pl.ds(x_ * XR, XR)], got.at[g, i], s_x.at[g, i], r_x.at[g, i], x_peer(i))

    def fold_x(g):
        for i in range(1, NX):
            arrive(got.at[g, i], s_x.at[g, i], r_x.at[g, i])
        total = part[g, pl.ds(x * XR, XR), :]
        for i in range(1, NX):
            total += got[g, i].astype(F32)
        for z_ in range(NZ):
            for yl_ in range(NYL):
                k = (yl_ * NZ + z_) * 4
                share[g, z_, yl_] = total[k : k + 4, :]
        land[g, z] = share[g, z]
        for i in range(1, NZ):
            send(share.at[g, (z + i) % NZ], land.at[g, z], s_f.at[g, i], r_f.at[g, i], z_peer(i))

    def give(g, yl_, yh_, slot, k):
        dev = (at(x, yl_, z), yh_ * NC + core)
        send(last.at[g, yl_], fin.at[slot], s_fin.at[k], r_fin.at[slot], dev)

    def fold_z(g):
        for i in range(1, NZ):
            arrive(land.at[g, (z - i + NZ) % NZ], s_f.at[g, i], r_f.at[g, i])
        for yl_ in range(NYL):
            total = land[g, 0, yl_]
            for z_ in range(1, NZ):
                total += land[g, z_, yl_]
            last[g, yl_] = total
        if g < 2:
            give(g, 1 - yl, yh, g, g)
        else:
            for yl_ in range(NYL):
                yh_ = (away_yh, before, after)[g - 2]
                give(g, yl_, yh_, g * 2 - 2 + yl, g * 2 - 2 + yl_)

    drain(9)

    @pl.when(jnp.logical_not(own_head))
    def _():
        head_copy(0).wait_send()

    for j in range(NJ):
        arrive(half.at[1 - core, j], s_hc.at[j, 0], r_hc.at[j, 0])
    multiply(0, [wide(half, core, j) for j in range(NJ)], lambda c: [wide(half, c, j) for j in range(NJ)])
    for j in (NJ - 2, NJ - 1):
        pass_near(j)
    for j in range(NJ):
        for s in range(2):
            arrive(near.at[s, 1 - core, j], s_hc.at[j, 1 + s], r_hc.at[j, 1 + s])
    for g, r, o in ((1, same, away), (2, away, same)):
        multiply(g, [wide(near, r, core, j) for j in range(NJ)], lambda c, o=o: [wide(near, o, c, j) for j in range(NJ)])
    fold_x(0)
    for j in range(NJ):
        for s in range(2):
            mine = far.at[s, core, j]
            arrive(mine, s_y.at[j, 2 + s], r_y.at[j, 2 + s])
            send(mine, mine, s_hc.at[j, 3 + s], r_hc.at[j, 3 + s], other)
    for j in range(NJ):
        for s in range(2):
            arrive(far.at[s, 1 - core, j], s_hc.at[j, 3 + s], r_hc.at[j, 3 + s])

    def pairs(s, c):
        return [jnp.concatenate([far[s, c, j], far[s, c, j + 1]], axis=1) for j in range(0, NJ, 2)]

    for g, s in ((3, 0), (4, 1)):
        multiply(g, pairs(s, core), lambda c, s=s: pairs(1 - s, c))
    fold_x(1)
    fold_x(2)
    fold_z(0)
    fold_x(3)
    fold_z(1)
    fold_x(4)
    fold_z(2)
    drain(21)
    fold_z(3)
    fold_z(4)

    def put(yh_, value):
        out_ref[:, pl.ds(pl.multiple_of(yh_ * GW, GW), GW)] = -0.25 * value

    def came(slot):
        arrive(fin.at[slot], s_fin.at[slot], r_fin.at[slot])

    for slot in range(4):
        came(slot)
    put(yh, last[0, yl] + fin[0])
    put(away_yh, last[1, yl] + fin[3 - yl])
    put(jnp.where(yl == 1, before, after), fin[1] + fin[2 + yl])
    for slot in range(4, 8):
        came(slot)
    put(across, (fin[4] + fin[5]) + (fin[6] + fin[7]))
    drain()


def local(three_centre, slot_index, slot_count, panel_last, panel_prev, panel_older):
    slots = jnp.transpose(slot_index, (0, 3, 1, 2))
    dma = pltpu.SemaphoreType.DMA
    hbm, vmem = pl.BlockSpec(memory_space=pltpu.HBM), pl.BlockSpec(memory_space=pltpu.VMEM)
    out = pl.pallas_call(
        kernel,
        out_shape=jax.ShapeDtypeStruct((4, NBLK * BLK), F32),
        in_specs=[hbm] * 6,
        out_specs=vmem,
        scratch_shapes=[
            pltpu.VMEM((SLOTS, RB, BLK, BLK), BF16),
            pltpu.VMEM((1, 3, 1, SLOTS), jnp.int32),
            pltpu.VMEM((1, 1), jnp.int32),
            pltpu.VMEM((3, 4, OCC), BF16),
            pltpu.VMEM((2, SLOTS, BLK), jnp.int32),
            pltpu.SMEM((2, SLOTS, BLK), jnp.int32),
            pltpu.VMEM((RB * ROWS, NBLK * BLK), BF16),
            pltpu.VMEM((16, BLK), BF16),
            pltpu.VMEM((4, 16, BLK), BF16),
            pltpu.VMEM((NJ, NRI, 2, 16, LW), BF16),
            pltpu.VMEM((NC, NJ, RB, ROWS, LW), BF16),
            pltpu.VMEM((2, NC, NJ, RB, ROWS, LW), BF16),
            pltpu.VMEM((2, NC, NJ, ROWS, LW), BF16),
            pltpu.VMEM((5, ROWS, GW), F32),
            pltpu.VMEM((5, ROWS, GW), BF16),
            pltpu.VMEM((5, NX, XR, GW), BF16),
            pltpu.VMEM((5, NZ, NYL, 4, GW), F32),
            pltpu.VMEM((5, NZ, NYL, 4, GW), F32),
            pltpu.VMEM((5, NYL, 4, GW), F32),
            pltpu.VMEM((8, 4, GW), F32),
            dma((7,)),
            dma((NYH,)), dma((4,)),
            dma((2, NZ)), dma((2, NZ)),
            dma((NX * NYL,)), dma((NX * NYL,)),
            dma((NX * NYL,)), dma((NX * NYL,)),
            dma((NJ,)), dma((NJ,)),
            dma((NJ, NYL, NX)), dma((NJ, NYL, NX)),
            dma((NJ,)), dma((NJ,)),
            dma((NJ, 4)), dma((NJ, 4)),
            dma((NJ, 5)), dma((NJ, 5)),
            dma((5, NX)), dma((5, NX)),
            dma((5, NZ)), dma((5, NZ)),
            dma((8,)), dma((8,)),
        ],
        compiler_params=pltpu.CompilerParams(
            collective_id=0, has_side_effects=True, vmem_limit_bytes=60 * 1024 * 1024
        ),
        cost_estimate=pl.CostEstimate(flops=2 << 30, bytes_accessed=3 << 20, transcendentals=0),
    )(three_centre[0, 0], slots, slot_count, panel_last, panel_prev, panel_older)
    return out[None, None]


def solution(mesh):
    return jax.shard_map(
        local,
        mesh=mesh,
        in_specs=(
            P("ri", "bas", None, None, None, None),
            P("ri", "bas", None, None),
            P("ri", "bas"),
            P(("ri", "bas"), None),
            P(("ri", "bas"), None),
            P(("ri", "bas"), None),
        ),
        out_specs=P("bas", "ri", None, None),
        check_vma=False,
    )
```

```python
import jax
import jax.numpy as jnp
from jax import lax
from jax.experimental import pallas as pl
from jax.experimental.pallas import tpu as pltpu
from jax.sharding import PartitionSpec as P

MESH = pl.DeviceIdType.MESH
BF16, F32 = jnp.bfloat16, jnp.float32

BLK = 128
NBLK = 16
OCC = 512
RB = 2
SLOTS = 32
ROWS = 256
NX, NYL, NZ, NYH, NC = 4, 2, 8, 4, 2
NRI = NX * NYL * NZ
NBAS = NYH * NC
NJ = 4
LW = OCC // NJ
XR = ROWS // NX
GW = 512


def kernel(
    t_hbm, slots_hbm, count_hbm, last_hbm, prev_hbm, older_hbm, out_ref,
    t_v, slots_v, count_v, panels_v, table_v, table, dense, pred, heads, panel, half, near, far,
    part, sent, got, share, land, share_b, land_b, last, fin,
    in_sem,
    s_head, r_head, s_z, r_z, s_xy, r_xy, s_lc, r_lc, s_pair, r_pair, s_line, r_line, s_core, r_core,
    s_y, r_y, s_hc, r_hc, s_x, r_x, s_f, r_f, s_fin, r_fin,
):
    ri, bas = lax.axis_index("ri"), lax.axis_index("bas")
    x, yl, z = ri // (NYL * NZ), (ri // NZ) % NYL, ri % NZ
    yh, core = bas // NC, bas % NC
    line = x * NYL + yl
    other = (ri, yh * NC + 1 - core)
    head_core = bas // 4
    head_slot = bas % 4

    def at(x_, yl_, z_):
        return (x_ * NYL + yl_) * NZ + z_

    def head_target(i):
        return (ri, ((yh + i) % NYH) * NC + head_core)

    def z_peer(i):
        return (at(x, yl, (z + i) % NZ), bas)

    def x_peer(i):
        return (at((x + i) % NX, yl, z), bas)

    def xy_peer(i):
        return (at((x + i // NYL) % NX, (yl + i % NYL) % NYL, z), bas)

    y = yh * NYL + yl

    def y_chip(d):
        y_ = (y + d + NYL * NYH) % (NYL * NYH)
        return (at(x, y_ % NYL, z), (y_ // NYL) * NC + core)

    pair = (at(x, 1 - yl, z), bas)
    started = []

    def remote(src, dst, ssem, rsem, dev):
        return pltpu.make_async_remote_copy(
            src_ref=src, dst_ref=dst, send_sem=ssem, recv_sem=rsem, device_id=dev, device_id_type=MESH
        )

    def send(src, dst, ssem, rsem, dev):
        copy = remote(src, dst, ssem, rsem, dev)
        copy.start()
        started.append(copy)

    def drain(keep=0):
        while len(started) > keep:
            started.pop(0).wait_send()

    def arrive(dst, ssem, rsem):
        remote(dst, dst, ssem, rsem, other).wait_recv()

    loads = [
        pltpu.make_async_copy(src, dst, in_sem.at[i])
        for i, (src, dst) in enumerate((
            (last_hbm, panels_v.at[0]), (prev_hbm, panels_v.at[1]), (older_hbm, panels_v.at[2]),
            (slots_hbm, slots_v), (count_hbm, count_v), (t_hbm, t_v),
        ))
    ]
    for copy in loads[:3]:
        copy.start()

    barrier = pltpu.get_barrier_semaphore()

    peers = [(ri, (bas + i) % NBAS) for i in range(1, NBAS)]
    peers += [z_peer(i) for i in range(1, NZ)]
    peers += [xy_peer(i) for i in range(1, NX * NYL)]
    for dev in peers:
        pl.semaphore_signal(barrier, inc=1, device_id=dev, device_id_type=MESH)

    for copy in loads[:3]:
        copy.wait()
    panels = [panels_v[i].astype(F32) for i in range(3)]
    mixed = 2.5 * panels[0] - 2.0 * panels[1] + 0.5 * panels[2]
    packed = jnp.concatenate([mixed[:, j * LW : (j + 1) * LW] for j in range(NJ)], axis=0).astype(BF16)
    pred[...] = packed
    own_head = core == head_core

    @pl.when(own_head)
    def _():
        heads[head_slot] = packed

    pl.semaphore_wait(barrier, len(peers))

    def head_copy(i):
        return remote(pred, heads.at[head_slot], s_head.at[i], r_head.at[head_slot], head_target(i))

    for i in range(1, NYH):
        copy = head_copy(i)
        copy.start()
        started.append(copy)

    @pl.when(jnp.logical_not(own_head))
    def _():
        head_copy(0).start()

    for copy in loads[3:]:
        copy.start()

    loads[3].wait()
    loads[4].wait()
    key = slots_v[0, 1] * NBLK + slots_v[0, 2]
    slot = lax.broadcasted_iota(jnp.int32, (SLOTS, SLOTS), 1)
    hit = lax.broadcasted_iota(jnp.int32, (SLOTS, SLOTS), 0) == key
    used = hit & (slot < count_v[...])
    inv = jnp.max(jnp.where(hit, slot, 0), axis=1, keepdims=True)
    live = jnp.sum(jnp.where(used, 1, 0), axis=1, keepdims=True)
    table_v[0] = jnp.broadcast_to(inv, (SLOTS, BLK))
    table_v[1] = jnp.broadcast_to(live, (SLOTS, BLK))
    copy = pltpu.make_async_copy(table_v, table, in_sem.at[6])
    copy.start()
    copy.wait()
    loads[5].wait()
    for u in range(ROWS // BLK):
        for v in range(NBLK):
            k = u * NBLK + v
            block = t_v[table[0, k, 0]]
            block = jnp.where(table[1, k, 0] != 0, block, jnp.zeros_like(block))
            for p in range(RB):
                dense[pl.ds(p * ROWS + u * BLK, BLK), pl.ds(v * BLK, BLK)] = block[p]

    for k in range(4):
        @pl.when(jnp.logical_not(own_head & (head_slot == k)))
        def _():
            arrive(heads.at[k], s_head.at[0], r_head.at[k])
    rows = [heads[k].astype(F32) for k in range(4)]
    for j in range(NJ):
        tile = jnp.concatenate([r[j * 4 : j * 4 + 4, :] for r in rows], axis=0)
        panel[j, ri, core] = tile.astype(BF16)

    parts = (pl.ds(0, 1), pl.ds(1, NJ - 1))
    for k, part_ in enumerate(parts):
        mine = panel.at[part_, ri, core]
        for i in (4, 3, 5, 2, 6, 1, 7):
            send(mine, mine, s_z.at[k, i], r_z.at[k, i], z_peer(i))

    def arrive_z(k):
        for i in range(1, NZ):
            src = at(x, yl, (z - i + NZ) % NZ)
            arrive(panel.at[parts[k], src, core], s_z.at[k, i], r_z.at[k, i])

    arrive_z(0)

    def line_of(j, line_):
        return panel.at[j, pl.ds(line_ * NZ, NZ), core]

    pair_line = x * NYL + 1 - yl
    def pass_core(line_):
        mine = line_of(0, line_)
        send(mine, mine, s_lc.at[line_], r_lc.at[line_], other)

    mine = line_of(0, line)
    for i in (5, 4, 3, 7, 2, 6, 1):
        send(mine, mine, s_xy.at[i], r_xy.at[i], xy_peer(i))
    pass_core(line)
    arrive_z(1)
    for j in range(1, NJ):
        mine = line_of(j, line)
        send(mine, mine, s_pair.at[j], r_pair.at[j], pair)

    def pass_own(j):
        mine = line_of(j, line)
        for i in range(1, NX):
            send(mine, mine, s_line.at[j, 0, i], r_line.at[j, 0, i], x_peer(i))

    def pass_pair(j):
        mine = line_of(j, pair_line)
        arrive(mine, s_pair.at[j], r_pair.at[j])
        for i in range(1, NX):
            send(mine, mine, s_line.at[j, 1, i], r_line.at[j, 1, i], x_peer(i))

    before, after = (yh - 1 + NYH) % NYH, (yh + 1) % NYH
    across = (yh + 2) % NYH

    def pass_near(j):
        for s in range(2):
            mine = near.at[s, core, j]
            arrive(mine, s_y.at[j, s], r_y.at[j, s])
            send(mine, mine, s_hc.at[j, 1 + s], r_hc.at[j, 1 + s], other)

    def pass_far(j):
        for s in range(2):
            d = 1 - 2 * s
            p = ((y + d + NYL * NYH) % (NYL * NYH)) // 4
            send(near.at[s, core, j, p], far.at[s, core, j], s_y.at[j, 2 + s], r_y.at[j, 2 + s], y_chip(d))

    for j in range(NJ):
        if j == 0:
            for i in (1, 2, 6, 3, 7, 4, 5):
                line_ = ((x - i // NYL + NX) % NX) * NYL + (yl + i % NYL) % NYL
                arrive(line_of(0, line_), s_xy.at[i], r_xy.at[i])
                pass_core(line_)
                if i == 6:
                    pass_own(1)
            pass_pair(1)
        else:
            for i in range(1, NX):
                x_ = (x - i + NX) % NX
                arrive(line_of(j, x_ * NYL + yl), s_line.at[j, 0, i], r_line.at[j, 0, i])
                arrive(line_of(j, x_ * NYL + 1 - yl), s_line.at[j, 1, i], r_line.at[j, 1, i])
        if j + 2 < NJ:
            pass_own(j + 2)
            pass_pair(j + 2)
        if j == 0:
            for line_ in range(NX * NYL):
                arrive(panel.at[0, pl.ds(line_ * NZ, NZ), 1 - core], s_lc.at[line_], r_lc.at[line_])
        else:
            mine = panel.at[j, :, core]
            send(mine, mine, s_core.at[j], r_core.at[j], other)
            arrive(panel.at[j, :, 1 - core], s_core.at[j], r_core.at[j])
        columns = panel[j].reshape(NBLK * BLK, LW)
        rows = jnp.dot(dense[...], columns, preferred_element_type=F32).astype(BF16)
        for p in range(RB):
            half[core, j, p] = rows[p * ROWS : (p + 1) * ROWS, :]
        mine = half.at[core, j]
        send(mine, near.at[0, core, j], s_y.at[j, 0], r_y.at[j, 0], y_chip(1))
        send(mine, near.at[1, core, j], s_y.at[j, 1], r_y.at[j, 1], y_chip(-1))
        send(mine, mine, s_hc.at[j, 0], r_hc.at[j, 0], other)
        if j >= 2:
            pass_near(j - 2)

    same, away = 1 - yl, yl
    away_yh = jnp.where(yl == 1, after, before)

    def wide(ref, *at_):
        return jnp.concatenate([ref[(*at_, p)] for p in range(RB)], axis=1)

    def multiply(g, rows, columns):
        for c in range(NC):
            total = jnp.zeros((ROWS, ROWS), F32)
            for lhs, rhs in zip(rows, columns(c), strict=True):
                total += lax.dot_general(lhs, rhs, (((1,), (1,)), ((), ())), preferred_element_type=F32)
            part[g, :, c * ROWS : (c + 1) * ROWS] = total
            sent[g, :, c * ROWS : (c + 1) * ROWS] = total.astype(BF16)
        for i in range(1, NX):
            x_ = (x + i) % NX
            send(sent.at[g, pl.ds(x_ * XR, XR)], got.at[g, i], s_x.at[g, i], r_x.at[g, i], x_peer(i))

    def fold_x(g):
        for i in range(1, NX):
            arrive(got.at[g, i], s_x.at[g, i], r_x.at[g, i])
        total = part[g, pl.ds(x * XR, XR), :]
        for i in range(1, NX):
            total += got[g, i].astype(F32)
        for z_ in range(NZ):
            pieces = [total[(yl_ * NZ + z_) * 4 : (yl_ * NZ + z_) * 4 + 4, :] for yl_ in range(NYL)]
            if g == 0:
                for yl_ in range(NYL):
                    share[z_, yl_] = pieces[yl_]
            else:
                tile = jnp.concatenate([p[:, h * 256 : h * 256 + 256] for h in range(2) for p in pieces], axis=0)
                share_b[g - 1, z_] = tile.astype(BF16)
        src, dst = (share, land) if g == 0 else (share_b.at[g - 1], land_b.at[g - 1])
        dst[z] = src[z]
        for i in (4, 3, 5, 2, 6, 1, 7):
            send(src.at[(z + i) % NZ], dst.at[z], s_f.at[g, i], r_f.at[g, i], z_peer(i))

    def give(g, yl_, yh_, slot, k):
        dev = (at(x, yl_, z), yh_ * NC + core)
        send(last.at[g, yl_], fin.at[slot], s_fin.at[k], r_fin.at[slot], dev)

    def fold_z(g):
        dst = land if g == 0 else land_b.at[g - 1]
        for i in range(1, NZ):
            arrive(dst.at[(z - i + NZ) % NZ], s_f.at[g, i], r_f.at[g, i])
        total = dst[0].astype(F32)
        for z_ in range(1, NZ):
            total += dst[z_].astype(F32)
        for yl_ in range(NYL):
            if g == 0:
                last[g, yl_] = total[yl_]
            else:
                for h in range(2):
                    k = (h * NYL + yl_) * 4
                    last[g, yl_, :, h * 256 : h * 256 + 256] = total[k : k + 4, :]
        if g < 2:
            give(g, 1 - yl, yh, g, g)
        else:
            for yl_ in range(NYL):
                yh_ = (away_yh, before, after)[g - 2]
                give(g, yl_, yh_, g * 2 - 2 + yl, g * 2 - 2 + yl_)

    drain(9)

    @pl.when(jnp.logical_not(own_head))
    def _():
        head_copy(0).wait_send()

    for j in range(NJ):
        arrive(half.at[1 - core, j], s_hc.at[j, 0], r_hc.at[j, 0])
    multiply(0, [wide(half, core, j) for j in range(NJ)], lambda c: [wide(half, c, j) for j in range(NJ)])
    pass_near(NJ - 2)
    for j in range(NJ - 1):
        pass_far(j)
    pass_near(NJ - 1)
    pass_far(NJ - 1)
    for j in range(NJ):
        for s in range(2):
            arrive(near.at[s, 1 - core, j], s_hc.at[j, 1 + s], r_hc.at[j, 1 + s])
    for g, r, o in ((1, same, away), (2, away, same)):
        multiply(g, [wide(near, r, core, j) for j in range(NJ)], lambda c, o=o: [wide(near, o, c, j) for j in range(NJ)])
    fold_x(0)
    for j in range(NJ):
        for s in range(2):
            mine = far.at[s, core, j]
            arrive(mine, s_y.at[j, 2 + s], r_y.at[j, 2 + s])
            send(mine, mine, s_hc.at[j, 3 + s], r_hc.at[j, 3 + s], other)
    for j in range(NJ):
        for s in range(2):
            arrive(far.at[s, 1 - core, j], s_hc.at[j, 3 + s], r_hc.at[j, 3 + s])

    def pairs(s, c):
        return [jnp.concatenate([far[s, c, j], far[s, c, j + 1]], axis=1) for j in range(0, NJ, 2)]

    for g, s in ((3, 0), (4, 1)):
        multiply(g, pairs(s, core), lambda c, s=s: pairs(1 - s, c))
    fold_x(1)
    fold_x(2)
    fold_z(0)
    fold_x(3)
    fold_z(1)
    fold_x(4)
    fold_z(2)
    drain(21)
    fold_z(3)
    fold_z(4)

    def put(yh_, value):
        out_ref[:, pl.ds(pl.multiple_of(yh_ * GW, GW), GW)] = -0.25 * value

    def came(slot):
        arrive(fin.at[slot], s_fin.at[slot], r_fin.at[slot])

    for slot in range(4):
        came(slot)
    put(yh, last[0, yl] + fin[0])
    put(away_yh, last[1, yl] + fin[3 - yl])
    put(jnp.where(yl == 1, before, after), fin[1] + fin[2 + yl])
    for slot in range(4, 8):
        came(slot)
    put(across, (fin[4] + fin[5]) + (fin[6] + fin[7]))
    drain()


def local(three_centre, slot_index, slot_count, panel_last, panel_prev, panel_older):
    slots = jnp.transpose(slot_index, (0, 3, 1, 2))
    dma = pltpu.SemaphoreType.DMA
    hbm, vmem = pl.BlockSpec(memory_space=pltpu.HBM), pl.BlockSpec(memory_space=pltpu.VMEM)
    out = pl.pallas_call(
        kernel,
        out_shape=jax.ShapeDtypeStruct((4, NBLK * BLK), F32),
        in_specs=[hbm] * 6,
        out_specs=vmem,
        scratch_shapes=[
            pltpu.VMEM((SLOTS, RB, BLK, BLK), BF16),
            pltpu.VMEM((1, 3, 1, SLOTS), jnp.int32),
            pltpu.VMEM((1, 1), jnp.int32),
            pltpu.VMEM((3, 4, OCC), BF16),
            pltpu.VMEM((2, SLOTS, BLK), jnp.int32),
            pltpu.SMEM((2, SLOTS, BLK), jnp.int32),
            pltpu.VMEM((RB * ROWS, NBLK * BLK), BF16),
            pltpu.VMEM((16, BLK), BF16),
            pltpu.VMEM((4, 16, BLK), BF16),
            pltpu.VMEM((NJ, NRI, 2, 16, LW), BF16),
            pltpu.VMEM((NC, NJ, RB, ROWS, LW), BF16),
            pltpu.VMEM((2, NC, NJ, RB, ROWS, LW), BF16),
            pltpu.VMEM((2, NC, NJ, ROWS, LW), BF16),
            pltpu.VMEM((5, ROWS, GW), F32),
            pltpu.VMEM((5, ROWS, GW), BF16),
            pltpu.VMEM((5, NX, XR, GW), BF16),
            pltpu.VMEM((NZ, NYL, 4, GW), F32),
            pltpu.VMEM((NZ, NYL, 4, GW), F32),
            pltpu.VMEM((4, NZ, 16, 256), BF16),
            pltpu.VMEM((4, NZ, 16, 256), BF16),
            pltpu.VMEM((5, NYL, 4, GW), F32),
            pltpu.VMEM((8, 4, GW), F32),
            dma((7,)),
            dma((NYH,)), dma((4,)),
            dma((2, NZ)), dma((2, NZ)),
            dma((NX * NYL,)), dma((NX * NYL,)),
            dma((NX * NYL,)), dma((NX * NYL,)),
            dma((NJ,)), dma((NJ,)),
            dma((NJ, NYL, NX)), dma((NJ, NYL, NX)),
            dma((NJ,)), dma((NJ,)),
            dma((NJ, 4)), dma((NJ, 4)),
            dma((NJ, 5)), dma((NJ, 5)),
            dma((5, NX)), dma((5, NX)),
            dma((5, NZ)), dma((5, NZ)),
            dma((8,)), dma((8,)),
        ],
        compiler_params=pltpu.CompilerParams(
            collective_id=0, has_side_effects=True, vmem_limit_bytes=60 * 1024 * 1024
        ),
        cost_estimate=pl.CostEstimate(flops=2 << 30, bytes_accessed=3 << 20, transcendentals=0),
    )(three_centre[0, 0], slots, slot_count, panel_last, panel_prev, panel_older)
    return out[None, None]


def solution(mesh):
    return jax.shard_map(
        local,
        mesh=mesh,
        in_specs=(
            P("ri", "bas", None, None, None, None),
            P("ri", "bas", None, None),
            P("ri", "bas"),
            P(("ri", "bas"), None),
            P(("ri", "bas"), None),
            P(("ri", "bas"), None),
        ),
        out_specs=P("bas", "ri", None, None),
        check_vma=False,
    )
```

```python
import jax
import jax.numpy as jnp
from jax import lax
from jax.experimental import pallas as pl
from jax.experimental.pallas import tpu as pltpu
from jax.sharding import PartitionSpec as P

MESH = pl.DeviceIdType.MESH
BF16, F32 = jnp.bfloat16, jnp.float32

BLK = 128
NBLK = 16
OCC = 512
RB = 2
SLOTS = 32
ROWS = 256
NX, NYL, NZ, NYH, NC = 4, 2, 8, 4, 2
NRI = NX * NYL * NZ
NBAS = NYH * NC
NJ = 4
LW = OCC // NJ
XR = ROWS // NX
GW = 512


def kernel(
    t_hbm, slots_hbm, count_hbm, last_hbm, prev_hbm, older_hbm, out_ref,
    t_v, slots_v, count_v, panels_v, table_v, table, dense, pred, heads, panel, half, near, far,
    part, sent, got, share, land, share_b, land_b, share_c, land_c, last, fin,
    in_sem,
    s_head, r_head, s_z, r_z, s_xy, r_xy, s_lc, r_lc, s_pair, r_pair, s_line, r_line, s_core, r_core,
    s_y, r_y, s_hc, r_hc, s_x, r_x, s_f, r_f, s_fin, r_fin, s_c, r_c,
):
    ri, bas = lax.axis_index("ri"), lax.axis_index("bas")
    x, yl, z = ri // (NYL * NZ), (ri // NZ) % NYL, ri % NZ
    yh, core = bas // NC, bas % NC

    def ring(v, n):
        return [v] + [jnp.where(v + i >= n, v + i - n, v + i) for i in range(1, n)]

    xs, yls, zs, yhs = ring(x, NX), [yl, 1 - yl], ring(z, NZ), ring(yh, NYH)
    line = x * NYL + yl
    other = (ri, yh * NC + 1 - core)
    head_core = bas // 4
    head_slot = bas % 4

    def at(x_, yl_, z_):
        return (x_ * NYL + yl_) * NZ + z_

    def head_target(i):
        return (ri, yhs[i % NYH] * NC + head_core)

    def z_peer(i):
        return (at(x, yl, zs[i]), bas)

    def x_peer(i):
        return (at(xs[i], yl, z), bas)

    def xy_peer(i):
        return (at(xs[i // NYL], yls[i % NYL], z), bas)

    next_yh, prev_yh = jnp.where(yl == 1, yhs[1], yh), jnp.where(yl == 1, yh, yhs[3])
    next_chip = (at(x, 1 - yl, z), next_yh * NC + core)
    prev_chip = (at(x, 1 - yl, z), prev_yh * NC + core)

    pair = (at(x, 1 - yl, z), bas)
    started = []

    def remote(src, dst, ssem, rsem, dev):
        return pltpu.make_async_remote_copy(
            src_ref=src, dst_ref=dst, send_sem=ssem, recv_sem=rsem, device_id=dev, device_id_type=MESH
        )

    def send(src, dst, ssem, rsem, dev):
        copy = remote(src, dst, ssem, rsem, dev)
        copy.start()
        started.append(copy)

    def drain(keep=0):
        while len(started) > keep:
            started.pop(0).wait_send()

    def arrive(dst, ssem, rsem):
        remote(dst, dst, ssem, rsem, other).wait_recv()

    loads = [
        pltpu.make_async_copy(src, dst, in_sem.at[i])
        for i, (src, dst) in enumerate((
            (last_hbm, panels_v.at[0]), (prev_hbm, panels_v.at[1]), (older_hbm, panels_v.at[2]),
            (slots_hbm, slots_v), (count_hbm, count_v), (t_hbm, t_v),
        ))
    ]
    for copy in loads[:3]:
        copy.start()

    barrier = pltpu.get_barrier_semaphore()

    def greet(dev):
        pl.semaphore_signal(barrier, inc=1, device_id=dev, device_id_type=MESH)

    own_head = core == head_core
    for k in range(4):
        @pl.when(4 * core + k != bas)
        def _():
            greet((ri, 4 * core + k))

    @pl.when(jnp.logical_not(own_head))
    def _():
        greet(other)

    peers = [z_peer(i) for i in range(1, NZ)]
    peers += [xy_peer(i) for i in range(1, NX * NYL)]
    for dev in peers:
        greet(dev)

    for copy in loads[:3]:
        copy.wait()
    panels = [panels_v[i].astype(F32) for i in range(3)]
    mixed = 2.5 * panels[0] - 2.0 * panels[1] + 0.5 * panels[2]
    packed = jnp.concatenate([mixed[:, j * LW : (j + 1) * LW] for j in range(NJ)], axis=0).astype(BF16)
    pred[...] = packed
    @pl.when(own_head)
    def _():
        heads[head_slot] = packed

    pl.semaphore_wait(barrier, 4 + len(peers))

    def head_copy(i):
        return remote(pred, heads.at[head_slot], s_head.at[i], r_head.at[head_slot], head_target(i))

    for i in range(1, NYH):
        copy = head_copy(i)
        copy.start()
        started.append(copy)

    @pl.when(jnp.logical_not(own_head))
    def _():
        head_copy(0).start()

    for copy in loads[3:]:
        copy.start()

    loads[3].wait()
    loads[4].wait()
    key = slots_v[0, 1] * NBLK + slots_v[0, 2]
    slot = lax.broadcasted_iota(jnp.int32, (SLOTS, SLOTS), 1)
    hit = lax.broadcasted_iota(jnp.int32, (SLOTS, SLOTS), 0) == key
    used = hit & (slot < count_v[...])
    inv = jnp.max(jnp.where(hit, slot, 0), axis=1, keepdims=True)
    live = jnp.sum(jnp.where(used, 1, 0), axis=1, keepdims=True)
    table_v[0] = jnp.broadcast_to(inv, (SLOTS, BLK))
    table_v[1] = jnp.broadcast_to(live, (SLOTS, BLK))
    copy = pltpu.make_async_copy(table_v, table, in_sem.at[6])
    copy.start()
    copy.wait()
    loads[5].wait()
    for u in range(ROWS // BLK):
        for v in range(NBLK):
            k = u * NBLK + v
            block = t_v[table[0, k, 0]]
            block = jnp.where(table[1, k, 0] != 0, block, jnp.zeros_like(block))
            for p in range(RB):
                dense[pl.ds(p * ROWS + u * BLK, BLK), pl.ds(v * BLK, BLK)] = block[p]

    for k in range(4):
        @pl.when(jnp.logical_not(own_head & (head_slot == k)))
        def _():
            arrive(heads.at[k], s_head.at[0], r_head.at[k])
    rows = [heads[k].astype(F32) for k in range(4)]
    for j in range(NJ):
        tile = jnp.concatenate([r[j * 4 : j * 4 + 4, :] for r in rows], axis=0)
        panel[j, ri, core] = tile.astype(BF16)

    parts = (pl.ds(0, 1), pl.ds(1, NJ - 1))
    for k, part_ in enumerate(parts):
        mine = panel.at[part_, ri, core]
        for i in (4, 3, 5, 2, 6, 1, 7):
            send(mine, mine, s_z.at[k, i], r_z.at[k, i], z_peer(i))

    def arrive_z(k):
        for i in range(1, NZ):
            src = at(x, yl, zs[NZ - i])
            arrive(panel.at[parts[k], src, core], s_z.at[k, i], r_z.at[k, i])

    arrive_z(0)

    def line_of(j, line_):
        return panel.at[j, pl.ds(line_ * NZ, NZ), core]

    pair_line = x * NYL + 1 - yl
    def pass_core(line_):
        mine = line_of(0, line_)
        send(mine, mine, s_lc.at[line_], r_lc.at[line_], other)

    mine = line_of(0, line)
    for i in (5, 4, 3, 7, 2, 6, 1):
        send(mine, mine, s_xy.at[i], r_xy.at[i], xy_peer(i))
    pass_core(line)
    arrive_z(1)
    for j in range(1, NJ):
        mine = line_of(j, line)
        send(mine, mine, s_pair.at[j], r_pair.at[j], pair)

    def pass_own(j):
        mine = line_of(j, line)
        for i in (2, 1, 3):
            send(mine, mine, s_line.at[j, 0, i], r_line.at[j, 0, i], x_peer(i))

    def pass_pair(j):
        mine = line_of(j, pair_line)
        arrive(mine, s_pair.at[j], r_pair.at[j])
        for i in (2, 1, 3):
            send(mine, mine, s_line.at[j, 1, i], r_line.at[j, 1, i], x_peer(i))

    before, after, across = yhs[3], yhs[1], yhs[2]

    def pass_near(j):
        for s in range(2):
            mine = near.at[s, core, j]
            arrive(mine, s_y.at[j, s], r_y.at[j, s])
            send(mine, mine, s_hc.at[j, 1 + s], r_hc.at[j, 1 + s], other)

    def pass_far(j):
        for s in range(2):
            dev, p = ((next_chip, next_yh // 2), (prev_chip, prev_yh // 2))[s]
            send(near.at[s, core, j, p], far.at[s, core, j], s_y.at[j, 2 + s], r_y.at[j, 2 + s], dev)

    for j in range(NJ):
        if j == 0:
            for i in (1, 2, 6, 3, 7, 4, 5):
                line_ = xs[(NX - i // NYL) % NX] * NYL + yls[i % NYL]
                arrive(line_of(0, line_), s_xy.at[i], r_xy.at[i])
                pass_core(line_)
                if i == 6:
                    pass_own(1)
            pass_pair(1)
        else:
            for i in range(1, NX):
                x_ = xs[NX - i]
                arrive(line_of(j, x_ * NYL + yl), s_line.at[j, 0, i], r_line.at[j, 0, i])
                arrive(line_of(j, x_ * NYL + 1 - yl), s_line.at[j, 1, i], r_line.at[j, 1, i])
        if j + 2 < NJ:
            pass_own(j + 2)
            pass_pair(j + 2)
        if j == 0:
            for line_ in range(NX * NYL):
                arrive(panel.at[0, pl.ds(line_ * NZ, NZ), 1 - core], s_lc.at[line_], r_lc.at[line_])
        else:
            mine = panel.at[j, :, core]
            send(mine, mine, s_core.at[j], r_core.at[j], other)
            arrive(panel.at[j, :, 1 - core], s_core.at[j], r_core.at[j])
        columns = panel[j].reshape(NBLK * BLK, LW)
        rows = jnp.dot(dense[...], columns, preferred_element_type=F32).astype(BF16)
        for p in range(RB):
            half[core, j, p] = rows[p * ROWS : (p + 1) * ROWS, :]
        mine = half.at[core, j]
        send(mine, near.at[0, core, j], s_y.at[j, 0], r_y.at[j, 0], next_chip)
        send(mine, near.at[1, core, j], s_y.at[j, 1], r_y.at[j, 1], prev_chip)
        send(mine, mine, s_hc.at[j, 0], r_hc.at[j, 0], other)
        if j >= 2:
            pass_near(j - 2)

    same, away = 1 - yl, yl
    away_yh = jnp.where(yl == 1, after, before)

    def wide(ref, *at_):
        return jnp.concatenate([ref[(*at_, p)] for p in range(RB)], axis=1)

    def multiply(g, rows, columns):
        for c in range(NC):
            total = jnp.zeros((ROWS, ROWS), F32)
            for lhs, rhs in zip(rows, columns(c), strict=True):
                total += lax.dot_general(lhs, rhs, (((1,), (1,)), ((), ())), preferred_element_type=F32)
            part[g, :, c * ROWS : (c + 1) * ROWS] = total
            sent[g, :, c * ROWS : (c + 1) * ROWS] = total.astype(BF16)
        for i in (2, 1, 3):
            x_ = xs[i]
            send(sent.at[g, pl.ds(x_ * XR, XR)], got.at[g, i], s_x.at[g, i], r_x.at[g, i], x_peer(i))

    def fold_x(g):
        for i in range(1, NX):
            arrive(got.at[g, i], s_x.at[g, i], r_x.at[g, i])
        total = part[g, pl.ds(x * XR, XR), :]
        for i in range(1, NX):
            total += got[g, i].astype(F32)
        if g > 2:
            for k in range(NYL * NZ):
                piece = total[k * 4 : k * 4 + 4, :]
                tile = jnp.concatenate([piece[:, h * BLK : h * BLK + BLK] for h in range(4)], axis=0)
                share_c[g - 3, k // NZ, k % NZ] = tile.astype(BF16)
            yh_ = (before, after)[g - 3]
            for i in (4, 3, 5, 2, 6, 1, 7, 0):
                for yl_ in range(NYL):
                    z_ = zs[i]
                    dev = (at(x, yl_, z_), yh_ * NC + core)
                    send(share_c.at[g - 3, yl_, z_], land_c.at[g - 3, yl, z], s_c.at[g - 3, yl_, i], r_c.at[g - 3, yl, i], dev)
            return
        for z_ in range(NZ):
            pieces = [total[(yl_ * NZ + z_) * 4 : (yl_ * NZ + z_) * 4 + 4, :] for yl_ in range(NYL)]
            if g == 0:
                for yl_ in range(NYL):
                    share[z_, yl_] = pieces[yl_]
            else:
                tile = jnp.concatenate([p[:, h * 256 : h * 256 + 256] for h in range(2) for p in pieces], axis=0)
                share_b[g - 1, z_] = tile.astype(BF16)
        src, dst = (share, land) if g == 0 else (share_b.at[g - 1], land_b.at[g - 1])
        dst[z] = src[z]
        for i in (4, 3, 5, 2, 6, 1, 7):
            send(src.at[zs[i]], dst.at[z], s_f.at[g, i], r_f.at[g, i], z_peer(i))

    def give(g, yl_, yh_, slot, k):
        dev = (at(x, yl_, z), yh_ * NC + core)
        send(last.at[g, yl_], fin.at[slot], s_fin.at[k], r_fin.at[slot], dev)

    def fold_z(g):
        dst = land if g == 0 else land_b.at[g - 1]
        for i in range(1, NZ):
            arrive(dst.at[zs[(NZ - i) % NZ]], s_f.at[g, i], r_f.at[g, i])
        total = dst[0].astype(F32)
        for z_ in range(1, NZ):
            total += dst[z_].astype(F32)
        for yl_ in range(NYL):
            if g == 0:
                last[g, yl_] = total[yl_]
            else:
                for h in range(2):
                    k = (h * NYL + yl_) * 4
                    last[g, yl_, :, h * 256 : h * 256 + 256] = total[k : k + 4, :]
        if g < 2:
            give(g, 1 - yl, yh, g, g)
        else:
            for yl_ in range(NYL):
                give(g, yl_, away_yh, 2 + yl, 2 + yl_)

    drain(9)

    @pl.when(jnp.logical_not(own_head))
    def _():
        head_copy(0).wait_send()

    for j in range(NJ):
        arrive(half.at[1 - core, j], s_hc.at[j, 0], r_hc.at[j, 0])
    multiply(0, [wide(half, core, j) for j in range(NJ)], lambda c: [wide(half, c, j) for j in range(NJ)])
    pass_near(NJ - 2)
    for j in range(NJ - 1):
        pass_far(j)
    pass_near(NJ - 1)
    pass_far(NJ - 1)
    for j in range(NJ):
        for s in range(2):
            arrive(near.at[s, 1 - core, j], s_hc.at[j, 1 + s], r_hc.at[j, 1 + s])
    for g, r, o in ((1, same, away), (2, away, same)):
        multiply(g, [wide(near, r, core, j) for j in range(NJ)], lambda c, o=o: [wide(near, o, c, j) for j in range(NJ)])
    fold_x(0)
    for j in range(NJ):
        for s in range(2):
            mine = far.at[s, core, j]
            arrive(mine, s_y.at[j, 2 + s], r_y.at[j, 2 + s])
            send(mine, mine, s_hc.at[j, 3 + s], r_hc.at[j, 3 + s], other)
    for j in range(NJ):
        for s in range(2):
            arrive(far.at[s, 1 - core, j], s_hc.at[j, 3 + s], r_hc.at[j, 3 + s])

    def pairs(s, c):
        return [jnp.concatenate([far[s, c, j], far[s, c, j + 1]], axis=1) for j in range(0, NJ, 2)]

    for g, s in ((3, 0), (4, 1)):
        multiply(g, pairs(s, core), lambda c, s=s: pairs(1 - s, c))
    fold_x(1)
    fold_x(2)
    fold_z(0)
    fold_x(3)
    fold_x(4)
    fold_z(1)
    fold_z(2)
    drain()

    def put(yh_, value):
        out_ref[:, pl.ds(pl.multiple_of(yh_ * GW, GW), GW)] = -0.25 * value

    def came(slot):
        arrive(fin.at[slot], s_fin.at[slot], r_fin.at[slot])

    for slot in range(4):
        came(slot)
    put(yh, last[0, yl] + fin[0])
    put(away_yh, last[1, yl] + fin[3 - yl])
    put(jnp.where(yl == 1, before, after), fin[1] + fin[2 + yl])
    total = jnp.zeros((16, BLK), F32)
    for k in range(2):
        for i in range(NZ):
            for yl_ in range(NYL):
                arrive(land_c.at[k, yl_, zs[(NZ - i) % NZ]], s_c.at[k, yl_, i], r_c.at[k, yl_, i])
        for i in range(NZ):
            for yl_ in range(NYL):
                total += land_c[k, yl_, i].astype(F32)
    put(across, jnp.concatenate([total[h * 4 : h * 4 + 4, :] for h in range(4)], axis=1))
    drain()


def local(three_centre, slot_index, slot_count, panel_last, panel_prev, panel_older):
    slots = jnp.transpose(slot_index, (0, 3, 1, 2))
    dma = pltpu.SemaphoreType.DMA
    hbm, vmem = pl.BlockSpec(memory_space=pltpu.HBM), pl.BlockSpec(memory_space=pltpu.VMEM)
    out = pl.pallas_call(
        kernel,
        out_shape=jax.ShapeDtypeStruct((4, NBLK * BLK), F32),
        in_specs=[hbm] * 6,
        out_specs=vmem,
        scratch_shapes=[
            pltpu.VMEM((SLOTS, RB, BLK, BLK), BF16),
            pltpu.VMEM((1, 3, 1, SLOTS), jnp.int32),
            pltpu.VMEM((1, 1), jnp.int32),
            pltpu.VMEM((3, 4, OCC), BF16),
            pltpu.VMEM((2, SLOTS, BLK), jnp.int32),
            pltpu.SMEM((2, SLOTS, BLK), jnp.int32),
            pltpu.VMEM((RB * ROWS, NBLK * BLK), BF16),
            pltpu.VMEM((16, BLK), BF16),
            pltpu.VMEM((4, 16, BLK), BF16),
            pltpu.VMEM((NJ, NRI, 2, 16, LW), BF16),
            pltpu.VMEM((NC, NJ, RB, ROWS, LW), BF16),
            pltpu.VMEM((2, NC, NJ, RB, ROWS, LW), BF16),
            pltpu.VMEM((2, NC, NJ, ROWS, LW), BF16),
            pltpu.VMEM((5, ROWS, GW), F32),
            pltpu.VMEM((5, ROWS, GW), BF16),
            pltpu.VMEM((5, NX, XR, GW), BF16),
            pltpu.VMEM((NZ, NYL, 4, GW), F32),
            pltpu.VMEM((NZ, NYL, 4, GW), F32),
            pltpu.VMEM((2, NZ, 16, 256), BF16),
            pltpu.VMEM((2, NZ, 16, 256), BF16),
            pltpu.VMEM((2, NYL, NZ, 16, BLK), BF16),
            pltpu.VMEM((2, NYL, NZ, 16, BLK), BF16),
            pltpu.VMEM((3, NYL, 4, GW), F32),
            pltpu.VMEM((4, 4, GW), F32),
            dma((7,)),
            dma((NYH,)), dma((4,)),
            dma((2, NZ)), dma((2, NZ)),
            dma((NX * NYL,)), dma((NX * NYL,)),
            dma((NX * NYL,)), dma((NX * NYL,)),
            dma((NJ,)), dma((NJ,)),
            dma((NJ, NYL, NX)), dma((NJ, NYL, NX)),
            dma((NJ,)), dma((NJ,)),
            dma((NJ, 4)), dma((NJ, 4)),
            dma((NJ, 5)), dma((NJ, 5)),
            dma((5, NX)), dma((5, NX)),
            dma((3, NZ)), dma((3, NZ)),
            dma((4,)), dma((4,)),
            dma((2, NYL, NZ)), dma((2, NYL, NZ)),
        ],
        compiler_params=pltpu.CompilerParams(
            collective_id=0, has_side_effects=True, vmem_limit_bytes=60 * 1024 * 1024
        ),
        cost_estimate=pl.CostEstimate(flops=2 << 30, bytes_accessed=3 << 20, transcendentals=0),
    )(three_centre[0, 0], slots, slot_count, panel_last, panel_prev, panel_older)
    return out[None, None]


def solution(mesh):
    return jax.shard_map(
        local,
        mesh=mesh,
        in_specs=(
            P("ri", "bas", None, None, None, None),
            P("ri", "bas", None, None),
            P("ri", "bas"),
            P(("ri", "bas"), None),
            P(("ri", "bas"), None),
            P(("ri", "bas"), None),
        ),
        out_specs=P("bas", "ri", None, None),
        check_vma=False,
    )
```

```python
import jax
import jax.numpy as jnp
from jax import lax
from jax.experimental import pallas as pl
from jax.experimental.pallas import tpu as pltpu
from jax.sharding import PartitionSpec as P

MESH = pl.DeviceIdType.MESH
BF16, F32 = jnp.bfloat16, jnp.float32

BLK = 128
NBLK = 16
OCC = 512
RB = 2
SLOTS = 32
ROWS = 256
NX, NYL, NZ, NYH, NC = 4, 2, 8, 4, 2
NRI = NX * NYL * NZ
NBAS = NYH * NC
NJ = 4
LW = OCC // NJ
XR = ROWS // NX
GW = 512


def kernel(
    t_hbm, slots_hbm, count_hbm, mixed_hbm, out_ref,
    t_v, slots_v, count_v, table_v, table, dense, pred, heads, panel, half, near, far,
    part, sent, got, share, land, share_b, land_b, share_c, land_c, last, fin,
    in_sem,
    s_head, r_head, s_z, r_z, s_xy, r_xy, s_lc, r_lc, s_pair, r_pair, s_line, r_line, s_core, r_core,
    s_y, r_y, s_hc, r_hc, s_x, r_x, s_f, r_f, s_fin, r_fin, s_c, r_c,
):
    ri, bas = lax.axis_index("ri"), lax.axis_index("bas")
    x, yl, z = ri // (NYL * NZ), (ri // NZ) % NYL, ri % NZ
    yh, core = bas // NC, bas % NC

    def ring(v, n):
        return [v] + [jnp.where(v + i >= n, v + i - n, v + i) for i in range(1, n)]

    xs, yls, zs, yhs = ring(x, NX), [yl, 1 - yl], ring(z, NZ), ring(yh, NYH)
    line = x * NYL + yl
    other = (ri, yh * NC + 1 - core)
    head_core = bas // 4
    head_slot = bas % 4

    def at(x_, yl_, z_):
        return (x_ * NYL + yl_) * NZ + z_

    def head_target(i):
        return (ri, yhs[i % NYH] * NC + head_core)

    def z_peer(i):
        return (at(x, yl, zs[i]), bas)

    def x_peer(i):
        return (at(xs[i], yl, z), bas)

    def xy_peer(i):
        return (at(xs[i // NYL], yls[i % NYL], z), bas)

    next_yh, prev_yh = jnp.where(yl == 1, yhs[1], yh), jnp.where(yl == 1, yh, yhs[3])
    next_chip = (at(x, 1 - yl, z), next_yh * NC + core)
    prev_chip = (at(x, 1 - yl, z), prev_yh * NC + core)

    pair = (at(x, 1 - yl, z), bas)
    started = []

    def remote(src, dst, ssem, rsem, dev):
        return pltpu.make_async_remote_copy(
            src_ref=src, dst_ref=dst, send_sem=ssem, recv_sem=rsem, device_id=dev, device_id_type=MESH
        )

    def send(src, dst, ssem, rsem, dev):
        copy = remote(src, dst, ssem, rsem, dev)
        copy.start()
        started.append(copy)

    def drain(keep=0):
        while len(started) > keep:
            started.pop(0).wait_send()

    def arrive(dst, ssem, rsem):
        remote(dst, dst, ssem, rsem, other).wait_recv()

    loads = [
        pltpu.make_async_copy(src, dst, in_sem.at[i])
        for i, (src, dst) in enumerate((
            (mixed_hbm, pred), (slots_hbm, slots_v), (count_hbm, count_v), (t_hbm, t_v),
        ))
    ]
    for copy in loads[:1]:
        copy.start()

    barrier = pltpu.get_barrier_semaphore()

    def greet(dev):
        pl.semaphore_signal(barrier, inc=1, device_id=dev, device_id_type=MESH)

    own_head = core == head_core
    for k in range(4):
        @pl.when(4 * core + k != bas)
        def _():
            greet((ri, 4 * core + k))

    @pl.when(jnp.logical_not(own_head))
    def _():
        greet(other)

    peers = [z_peer(i) for i in range(1, NZ)]
    peers += [xy_peer(i) for i in range(1, NX * NYL)]
    for dev in peers:
        greet(dev)

    loads[0].wait()
    packed = pred[...]
    @pl.when(own_head)
    def _():
        heads[head_slot] = packed

    pl.semaphore_wait(barrier, 4 + len(peers))

    def head_copy(i):
        return remote(pred, heads.at[head_slot], s_head.at[i], r_head.at[head_slot], head_target(i))

    for i in range(1, NYH):
        copy = head_copy(i)
        copy.start()
        started.append(copy)

    @pl.when(jnp.logical_not(own_head))
    def _():
        head_copy(0).start()

    for copy in loads[1:]:
        copy.start()

    loads[1].wait()
    loads[2].wait()
    key = slots_v[0, 1] * NBLK + slots_v[0, 2]
    slot = lax.broadcasted_iota(jnp.int32, (SLOTS, SLOTS), 1)
    hit = lax.broadcasted_iota(jnp.int32, (SLOTS, SLOTS), 0) == key
    used = hit & (slot < count_v[...])
    inv = jnp.max(jnp.where(hit, slot, 0), axis=1, keepdims=True)
    live = jnp.sum(jnp.where(used, 1, 0), axis=1, keepdims=True)
    table_v[0] = jnp.broadcast_to(inv, (SLOTS, BLK))
    table_v[1] = jnp.broadcast_to(live, (SLOTS, BLK))
    copy = pltpu.make_async_copy(table_v, table, in_sem.at[4])
    copy.start()
    copy.wait()
    loads[3].wait()
    for u in range(ROWS // BLK):
        for v in range(NBLK):
            k = u * NBLK + v
            block = t_v[table[0, k, 0]]
            block = jnp.where(table[1, k, 0] != 0, block, jnp.zeros_like(block))
            for p in range(RB):
                dense[pl.ds(p * ROWS + u * BLK, BLK), pl.ds(v * BLK, BLK)] = block[p]

    for k in range(4):
        @pl.when(jnp.logical_not(own_head & (head_slot == k)))
        def _():
            arrive(heads.at[k], s_head.at[0], r_head.at[k])
    rows = [heads[k].astype(F32) for k in range(4)]
    for j in range(NJ):
        tile = jnp.concatenate([r[j * 4 : j * 4 + 4, :] for r in rows], axis=0)
        panel[j, ri, core] = tile.astype(BF16)

    parts = (pl.ds(0, 1), pl.ds(1, NJ - 1))
    for k, part_ in enumerate(parts):
        mine = panel.at[part_, ri, core]
        for i in (4, 3, 5, 2, 6, 1, 7):
            send(mine, mine, s_z.at[k, i], r_z.at[k, i], z_peer(i))

    def arrive_z(k):
        for i in range(1, NZ):
            src = at(x, yl, zs[NZ - i])
            arrive(panel.at[parts[k], src, core], s_z.at[k, i], r_z.at[k, i])

    arrive_z(0)

    def line_of(j, line_):
        return panel.at[j, pl.ds(line_ * NZ, NZ), core]

    pair_line = x * NYL + 1 - yl
    def pass_core(line_):
        mine = line_of(0, line_)
        send(mine, mine, s_lc.at[line_], r_lc.at[line_], other)

    mine = line_of(0, line)
    for i in (5, 4, 3, 7, 2, 6, 1):
        send(mine, mine, s_xy.at[i], r_xy.at[i], xy_peer(i))
    pass_core(line)
    arrive_z(1)
    for j in range(1, NJ):
        mine = line_of(j, line)
        send(mine, mine, s_pair.at[j], r_pair.at[j], pair)

    def pass_own(j):
        mine = line_of(j, line)
        for i in (2, 1, 3):
            send(mine, mine, s_line.at[j, 0, i], r_line.at[j, 0, i], x_peer(i))

    def pass_pair(j):
        mine = line_of(j, pair_line)
        arrive(mine, s_pair.at[j], r_pair.at[j])
        for i in (2, 1, 3):
            send(mine, mine, s_line.at[j, 1, i], r_line.at[j, 1, i], x_peer(i))

    before, after, across = yhs[3], yhs[1], yhs[2]

    def pass_near(j):
        for s in range(2):
            mine = near.at[s, core, j]
            arrive(mine, s_y.at[j, s], r_y.at[j, s])
            send(mine, mine, s_hc.at[j, 1 + s], r_hc.at[j, 1 + s], other)

    def pass_far(j):
        for s in range(2):
            dev, p = ((next_chip, next_yh // 2), (prev_chip, prev_yh // 2))[s]
            send(near.at[s, core, j, p], far.at[s, core, j], s_y.at[j, 2 + s], r_y.at[j, 2 + s], dev)

    for j in range(NJ):
        if j == 0:
            for i in (1, 2, 6, 3, 7, 4, 5):
                line_ = xs[(NX - i // NYL) % NX] * NYL + yls[i % NYL]
                arrive(line_of(0, line_), s_xy.at[i], r_xy.at[i])
                pass_core(line_)
                if i == 6:
                    pass_own(1)
            pass_pair(1)
        else:
            for i in range(1, NX):
                x_ = xs[NX - i]
                arrive(line_of(j, x_ * NYL + yl), s_line.at[j, 0, i], r_line.at[j, 0, i])
                arrive(line_of(j, x_ * NYL + 1 - yl), s_line.at[j, 1, i], r_line.at[j, 1, i])
        if j + 2 < NJ:
            pass_own(j + 2)
            pass_pair(j + 2)
        if j == 0:
            for line_ in range(NX * NYL):
                arrive(panel.at[0, pl.ds(line_ * NZ, NZ), 1 - core], s_lc.at[line_], r_lc.at[line_])
        else:
            mine = panel.at[j, :, core]
            send(mine, mine, s_core.at[j], r_core.at[j], other)
            arrive(panel.at[j, :, 1 - core], s_core.at[j], r_core.at[j])
        columns = panel[j].reshape(NBLK * BLK, LW)
        rows = jnp.dot(dense[...], columns, preferred_element_type=F32).astype(BF16)
        for p in range(RB):
            half[core, j, p] = rows[p * ROWS : (p + 1) * ROWS, :]
        mine = half.at[core, j]
        send(mine, near.at[0, core, j], s_y.at[j, 0], r_y.at[j, 0], next_chip)
        send(mine, near.at[1, core, j], s_y.at[j, 1], r_y.at[j, 1], prev_chip)
        send(mine, mine, s_hc.at[j, 0], r_hc.at[j, 0], other)
        if j >= 2:
            pass_near(j - 2)

    same, away = 1 - yl, yl
    away_yh = jnp.where(yl == 1, after, before)

    def wide(ref, *at_):
        return jnp.concatenate([ref[(*at_, p)] for p in range(RB)], axis=1)

    def multiply(g, rows, columns):
        for c in range(NC):
            total = jnp.zeros((ROWS, ROWS), F32)
            for lhs, rhs in zip(rows, columns(c), strict=True):
                total += lax.dot_general(lhs, rhs, (((1,), (1,)), ((), ())), preferred_element_type=F32)
            part[g, :, c * ROWS : (c + 1) * ROWS] = total
            sent[g, :, c * ROWS : (c + 1) * ROWS] = total.astype(BF16)
        for i in (2, 1, 3):
            x_ = xs[i]
            send(sent.at[g, pl.ds(x_ * XR, XR)], got.at[g, i], s_x.at[g, i], r_x.at[g, i], x_peer(i))

    def fold_x(g):
        for i in range(1, NX):
            arrive(got.at[g, i], s_x.at[g, i], r_x.at[g, i])
        total = part[g, pl.ds(x * XR, XR), :]
        for i in range(1, NX):
            total += got[g, i].astype(F32)
        if g > 2:
            for k in range(NYL * NZ):
                piece = total[k * 4 : k * 4 + 4, :]
                tile = jnp.concatenate([piece[:, h * BLK : h * BLK + BLK] for h in range(4)], axis=0)
                share_c[g - 3, k // NZ, k % NZ] = tile.astype(BF16)
            yh_ = (before, after)[g - 3]
            for i in (4, 3, 5, 2, 6, 1, 7, 0):
                for yl_ in range(NYL):
                    z_ = zs[i]
                    dev = (at(x, yl_, z_), yh_ * NC + core)
                    send(share_c.at[g - 3, yl_, z_], land_c.at[g - 3, yl, z], s_c.at[g - 3, yl_, i], r_c.at[g - 3, yl, i], dev)
            return
        for z_ in range(NZ):
            pieces = [total[(yl_ * NZ + z_) * 4 : (yl_ * NZ + z_) * 4 + 4, :] for yl_ in range(NYL)]
            if g == 0:
                for yl_ in range(NYL):
                    share[z_, yl_] = pieces[yl_]
            else:
                tile = jnp.concatenate([p[:, h * 256 : h * 256 + 256] for h in range(2) for p in pieces], axis=0)
                share_b[g - 1, z_] = tile.astype(BF16)
        src, dst = (share, land) if g == 0 else (share_b.at[g - 1], land_b.at[g - 1])
        dst[z] = src[z]
        for i in (4, 3, 5, 2, 6, 1, 7):
            send(src.at[zs[i]], dst.at[z], s_f.at[g, i], r_f.at[g, i], z_peer(i))

    def give(g, yl_, yh_, slot, k):
        dev = (at(x, yl_, z), yh_ * NC + core)
        send(last.at[g, yl_], fin.at[slot], s_fin.at[k], r_fin.at[slot], dev)

    def fold_z(g):
        dst = land if g == 0 else land_b.at[g - 1]
        for i in range(1, NZ):
            arrive(dst.at[zs[(NZ - i) % NZ]], s_f.at[g, i], r_f.at[g, i])
        total = dst[0].astype(F32)
        for z_ in range(1, NZ):
            total += dst[z_].astype(F32)
        for yl_ in range(NYL):
            if g == 0:
                last[g, yl_] = total[yl_]
            else:
                for h in range(2):
                    k = (h * NYL + yl_) * 4
                    last[g, yl_, :, h * 256 : h * 256 + 256] = total[k : k + 4, :]
        if g < 2:
            give(g, 1 - yl, yh, g, g)
        else:
            for yl_ in range(NYL):
                give(g, yl_, away_yh, 2 + yl, 2 + yl_)

    drain(9)

    @pl.when(jnp.logical_not(own_head))
    def _():
        head_copy(0).wait_send()

    for j in range(NJ):
        arrive(half.at[1 - core, j], s_hc.at[j, 0], r_hc.at[j, 0])
    multiply(0, [wide(half, core, j) for j in range(NJ)], lambda c: [wide(half, c, j) for j in range(NJ)])
    pass_near(NJ - 2)
    for j in range(NJ - 1):
        pass_far(j)
    pass_near(NJ - 1)
    pass_far(NJ - 1)
    for j in range(NJ):
        for s in range(2):
            arrive(near.at[s, 1 - core, j], s_hc.at[j, 1 + s], r_hc.at[j, 1 + s])
    for g, r, o in ((1, same, away), (2, away, same)):
        multiply(g, [wide(near, r, core, j) for j in range(NJ)], lambda c, o=o: [wide(near, o, c, j) for j in range(NJ)])
    fold_x(0)
    for j in range(NJ):
        for s in range(2):
            mine = far.at[s, core, j]
            arrive(mine, s_y.at[j, 2 + s], r_y.at[j, 2 + s])
            send(mine, mine, s_hc.at[j, 3 + s], r_hc.at[j, 3 + s], other)
    for j in range(NJ):
        for s in range(2):
            arrive(far.at[s, 1 - core, j], s_hc.at[j, 3 + s], r_hc.at[j, 3 + s])

    def pairs(s, c):
        return [jnp.concatenate([far[s, c, j], far[s, c, j + 1]], axis=1) for j in range(0, NJ, 2)]

    for g, s in ((3, 0), (4, 1)):
        multiply(g, pairs(s, core), lambda c, s=s: pairs(1 - s, c))
    fold_x(1)
    fold_x(2)
    fold_z(0)
    fold_x(3)
    fold_x(4)
    fold_z(1)
    fold_z(2)
    drain()

    def put(yh_, value):
        out_ref[:, pl.ds(pl.multiple_of(yh_ * GW, GW), GW)] = -0.25 * value

    def came(slot):
        arrive(fin.at[slot], s_fin.at[slot], r_fin.at[slot])

    for slot in range(4):
        came(slot)
    put(yh, last[0, yl] + fin[0])
    put(away_yh, last[1, yl] + fin[3 - yl])
    put(jnp.where(yl == 1, before, after), fin[1] + fin[2 + yl])
    total = jnp.zeros((16, BLK), F32)
    for k in range(2):
        for i in range(NZ):
            for yl_ in range(NYL):
                arrive(land_c.at[k, yl_, zs[(NZ - i) % NZ]], s_c.at[k, yl_, i], r_c.at[k, yl_, i])
        for i in range(NZ):
            for yl_ in range(NYL):
                total += land_c[k, yl_, i].astype(F32)
    put(across, jnp.concatenate([total[h * 4 : h * 4 + 4, :] for h in range(4)], axis=1))
    drain()


def local(three_centre, slot_index, slot_count, panel_last, panel_prev, panel_older):
    mixed = (
        2.5 * panel_last.astype(F32) - 2.0 * panel_prev.astype(F32) + 0.5 * panel_older.astype(F32)
    ).astype(BF16)
    mixed = jnp.transpose(mixed.reshape(4, NJ, LW), (1, 0, 2)).reshape(16, BLK)
    slots = jnp.transpose(slot_index, (0, 3, 1, 2))
    dma = pltpu.SemaphoreType.DMA
    hbm, vmem = pl.BlockSpec(memory_space=pltpu.HBM), pl.BlockSpec(memory_space=pltpu.VMEM)
    out = pl.pallas_call(
        kernel,
        out_shape=jax.ShapeDtypeStruct((4, NBLK * BLK), F32),
        in_specs=[hbm] * 4,
        out_specs=vmem,
        scratch_shapes=[
            pltpu.VMEM((SLOTS, RB, BLK, BLK), BF16),
            pltpu.VMEM((1, 3, 1, SLOTS), jnp.int32),
            pltpu.VMEM((1, 1), jnp.int32),
            pltpu.VMEM((2, SLOTS, BLK), jnp.int32),
            pltpu.SMEM((2, SLOTS, BLK), jnp.int32),
            pltpu.VMEM((RB * ROWS, NBLK * BLK), BF16),
            pltpu.VMEM((16, BLK), BF16),
            pltpu.VMEM((4, 16, BLK), BF16),
            pltpu.VMEM((NJ, NRI, 2, 16, LW), BF16),
            pltpu.VMEM((NC, NJ, RB, ROWS, LW), BF16),
            pltpu.VMEM((2, NC, NJ, RB, ROWS, LW), BF16),
            pltpu.VMEM((2, NC, NJ, ROWS, LW), BF16),
            pltpu.VMEM((5, ROWS, GW), F32),
            pltpu.VMEM((5, ROWS, GW), BF16),
            pltpu.VMEM((5, NX, XR, GW), BF16),
            pltpu.VMEM((NZ, NYL, 4, GW), F32),
            pltpu.VMEM((NZ, NYL, 4, GW), F32),
            pltpu.VMEM((2, NZ, 16, 256), BF16),
            pltpu.VMEM((2, NZ, 16, 256), BF16),
            pltpu.VMEM((2, NYL, NZ, 16, BLK), BF16),
            pltpu.VMEM((2, NYL, NZ, 16, BLK), BF16),
            pltpu.VMEM((3, NYL, 4, GW), F32),
            pltpu.VMEM((4, 4, GW), F32),
            dma((7,)),
            dma((NYH,)), dma((4,)),
            dma((2, NZ)), dma((2, NZ)),
            dma((NX * NYL,)), dma((NX * NYL,)),
            dma((NX * NYL,)), dma((NX * NYL,)),
            dma((NJ,)), dma((NJ,)),
            dma((NJ, NYL, NX)), dma((NJ, NYL, NX)),
            dma((NJ,)), dma((NJ,)),
            dma((NJ, 4)), dma((NJ, 4)),
            dma((NJ, 5)), dma((NJ, 5)),
            dma((5, NX)), dma((5, NX)),
            dma((3, NZ)), dma((3, NZ)),
            dma((4,)), dma((4,)),
            dma((2, NYL, NZ)), dma((2, NYL, NZ)),
        ],
        compiler_params=pltpu.CompilerParams(
            collective_id=0, has_side_effects=True, vmem_limit_bytes=60 * 1024 * 1024
        ),
        cost_estimate=pl.CostEstimate(flops=2 << 30, bytes_accessed=3 << 20, transcendentals=0),
    )(three_centre[0, 0], slots, slot_count, mixed)
    return out[None, None]


def solution(mesh):
    return jax.shard_map(
        local,
        mesh=mesh,
        in_specs=(
            P("ri", "bas", None, None, None, None),
            P("ri", "bas", None, None),
            P("ri", "bas"),
            P(("ri", "bas"), None),
            P(("ri", "bas"), None),
            P(("ri", "bas"), None),
        ),
        out_specs=P("bas", "ri", None, None),
        check_vma=False,
    )
```
